32 devices in a mesh: dom: 8 (over z, y), sub: 4 (over x, core).
Axes of the slice: x: 2, y: 2, z: 4, core: 2. Of those that a mesh axis runs over, the one named last changes fastest.
Arguments:
- segments: float32 [64, 9, 128], P(('dom', 'sub')), may hold values from -6 to 6
- stress: float32 [3, 3], replicated, may hold values from -3 to 3
- drag_coef: float32 [64, 128], P(('dom', 'sub')), may hold values from 0.5 to 4
- send_ids: int32 [32, 8, 1], P(('dom', 'sub')), may hold values from -1 to 1, as said below
- partner_ids: int32 [32, 8, 1], P(('dom', 'sub')), may hold values from 0 to 1
Outputs:
- positions: float32 [64, 3, 128], P(('dom', 'sub'))
- velocity: float32 [64, 3, 128], P(('dom', 'sub'))
The draws below stay inside these ranges and needn't reach their ends.
Inputs may be any that keep to these rules, and one draw needn't show every extreme that they name: `send_ids`: entry [d, p, s] names a block of device d, which goes in slot s to the device with dom index p and d's sub index; -1 marks an empty slot. Some device receives a block in every slot from every sender.
All inputs are finite; a program needn't handle non-finite values.
Results may differ from the reference program's by a relative error of at most 0.0003.
Values sent between devices are 32-bit elements; how exact they have to be, the bound alone decides.
A program may use at most 64 MiB of HBM per device.

```python
import math
import jax
import jax.numpy as jnp
from jax import lax

BLK = 128
NB_DEV = 2
SLOTS = 1
STEPS = 2
NBLOCKS = 64
N_DOM = 8
N_SUB = 4


def draw_send_ids(key, part):
    subkeys = jax.random.split(key, 4)
    device_count = N_DOM * N_SUB
    levels = jax.random.randint(subkeys[0], (device_count,), 1, 5)
    hottest = jax.random.randint(subkeys[1], (), 0, device_count)
    levels = jnp.where(jnp.arange(device_count, dtype=jnp.int32) == hottest, 8, levels)
    sender = jnp.arange(device_count, dtype=jnp.int32)[:, None, None]
    peer_index = jnp.arange(N_DOM, dtype=jnp.int32)[None, :, None]
    receiver = peer_index * N_SUB + sender % N_SUB
    receiver = jnp.broadcast_to(receiver, (device_count, N_DOM, SLOTS))
    rolled = jax.random.randint(subkeys[2], (device_count, N_DOM, SLOTS), 0, 8)
    filled = rolled < levels[receiver]
    block_ids = jax.random.randint(subkeys[3], (device_count, N_DOM, SLOTS), 0, NB_DEV)
    return jnp.where(filled, block_ids, -1).astype(jnp.int32)


def place_ends(entries, stream_key, smallest, largest):
    place = [jax.random.randint(jax.random.fold_in(stream_key, axis), (), 0, length) for axis, length in enumerate(entries.shape)]
    longest = entries.shape.index(max(entries.shape))
    next_to = place[:longest] + [(place[longest] + 1) % entries.shape[longest]] + place[longest + 1:]
    return entries.at[tuple(place)].set(smallest).at[tuple(next_to)].set(largest)


def block_scale(stream_key, extent, cuts, low, largest):
    def one(dim, blocks):
        draws = jax.random.uniform(jax.random.fold_in(jax.random.fold_in(stream_key, 6), dim), (blocks,), jnp.float32, low / len(cuts), largest / len(cuts))
        return jnp.repeat(jnp.exp(draws), extent[dim] // blocks).reshape((-1,) + (1,) * (len(extent) - dim - 1))

    gain = one(*cuts[0])
    for cut in cuts[1:]:
        gain = gain * one(*cut)
    return gain


def bell_draw(stream_key, shape, spread, limit, cuts=(), kind=jnp.bfloat16):
    result = spread * jax.random.normal(stream_key, shape, jnp.float32)
    if cuts:
        result = result * block_scale(stream_key, shape, cuts, -0.22, 0.18)
    return jnp.clip(result, -limit, limit).astype(kind)


def setup_inputs(seed: int = 0) -> dict:
    key_of = jax.random.split(jax.random.key(seed), 6)
    return {
        "segments": bell_draw(key_of[0], (NBLOCKS, 9, BLK), 1.0, 6.0, ((0, 32),), jnp.float32),
        "stress": bell_draw(key_of[1], (3, 3), 0.5, 3.0, (), jnp.float32),
        "drag_coef": jnp.clip(jnp.exp(math.log(4.0) - 2.0794415 * jax.random.uniform(key_of[2], (NBLOCKS, BLK), jnp.float32) ** block_scale(key_of[2], (NBLOCKS, BLK), ((0, 32),), -0.2, 0.2)), 0.5, 4.0),
        "send_ids": draw_send_ids(jax.random.fold_in(key_of[5], 71), 0),
        "partner_ids": place_ends(jax.random.randint(key_of[4], (N_DOM * N_SUB, N_DOM, SLOTS), 0, NB_DEV), jax.random.fold_in(key_of[4], 1), 0, NB_DEV - 1).astype(jnp.int32),
    }


COUPLE = 0.0625
CORE_SQUARE = 0.5
TENSION = 0.25
STEP_LENGTH = 1.0
EPSILON = 1e-06

def pair_terms(target, source):
    offsets = [target[..., component, :][..., :, None] - source[..., component, :][..., None, :] for component in range(3)]
    distance_sq = CORE_SQUARE + offsets[0] * offsets[0] + offsets[1] * offsets[1] + offsets[2] * offsets[2]
    inverse = lax.rsqrt(distance_sq)
    burgers_dot = target[..., 6, :][..., :, None] * source[..., 6, :][..., None, :]
    burgers_dot = burgers_dot + target[..., 7, :][..., :, None] * source[..., 7, :][..., None, :]
    burgers_dot = burgers_dot + target[..., 8, :][..., :, None] * source[..., 8, :][..., None, :]
    lines_dot = target[..., 3, :][..., :, None] * source[..., 3, :][..., None, :]
    lines_dot = lines_dot + target[..., 4, :][..., :, None] * source[..., 4, :][..., None, :]
    lines_dot = lines_dot + target[..., 5, :][..., :, None] * source[..., 5, :][..., None, :]
    weights = burgers_dot * lines_dot * inverse * inverse * inverse
    return (weights, offsets)

def force_on_target(weights, offsets):
    return jnp.stack([lax.optimization_barrier(jnp.sum(weights * offset_c, axis=-1)) for offset_c in offsets], axis=-2)

def force_on_source(weights, offsets):
    return jnp.stack([-lax.optimization_barrier(jnp.sum(weights * offset_c, axis=-2)) for offset_c in offsets], axis=-2)

def external_force(stress, line_vec, burgers):
    pulled = [stress[component, 0] * burgers[:, 0] + stress[component, 1] * burgers[:, 1] + stress[component, 2] * burgers[:, 2] for component in range(3)]
    first = pulled[1] * line_vec[:, 2] - pulled[2] * line_vec[:, 1]
    second = pulled[2] * line_vec[:, 0] - pulled[0] * line_vec[:, 2]
    third = pulled[0] * line_vec[:, 1] - pulled[1] * line_vec[:, 0]
    return jnp.stack([first, second, third], axis=1)

def chain_term(position):
    left_side = jnp.concatenate([position[..., :1], position[..., :-1]], axis=-1)
    right_side = jnp.concatenate([position[..., 1:], position[..., -1:]], axis=-1)
    return left_side + right_side - 2.0 * position

def group_forces(seg_state):
    group_blocks = N_SUB * NB_DEV
    grouped = seg_state.reshape(N_DOM, group_blocks, 9, BLK)

    def one_group(blocks):
        target = blocks.transpose(1, 0, 2).reshape(9, group_blocks * BLK)

        def add_block(running, source):
            weights, offsets = pair_terms(target, source)
            return (running + force_on_target(weights, offsets), None)
        running = lax.scan(add_block, jnp.zeros((3, group_blocks * BLK), jnp.float32), blocks)[0]
        return running.reshape(3, group_blocks, BLK).transpose(1, 0, 2)
    return lax.map(one_group, grouped).reshape(N_DOM * group_blocks, 3, BLK)

def cross_forces(seg_state, is_valid, source_block, target_block):
    pair_count = is_valid.shape[0]
    batch_size = math.gcd(pair_count, 64)
    source_ids = source_block.reshape(-1, batch_size)
    target_ids = target_block.reshape(-1, batch_size)
    keep_flags = is_valid.reshape(-1, batch_size)

    def one_batch(accum_force, pieces):
        src_rows, tgt_rows, keep_rows = pieces
        source = jnp.where(keep_rows[:, None, None], seg_state[src_rows], 0.0)
        target = seg_state[tgt_rows]
        weights, offsets = pair_terms(target, source)
        accum_force = accum_force.at[tgt_rows].add(force_on_target(weights, offsets))
        accum_force = accum_force.at[src_rows].add(force_on_source(weights, offsets))
        return (accum_force, None)
    start_force = jnp.zeros((seg_state.shape[0], 3, BLK), jnp.float32)
    return lax.scan(one_batch, start_force, (source_ids, target_ids, keep_flags))[0]

def reference(segments, stress, drag_coef, send_ids, partner_ids):
    position = segments[:, 0:3]
    line_vec = segments[:, 3:6]
    burgers = segments[:, 6:9]
    applied = external_force(stress, line_vec, burgers)
    device_count = N_DOM * N_SUB
    sender = jnp.arange(device_count, dtype=jnp.int32)[:, None, None]
    peer_index = jnp.arange(N_DOM, dtype=jnp.int32)[None, :, None]
    receiver = peer_index * N_SUB + sender % N_SUB
    is_valid = (send_ids >= 0).reshape(-1)
    source_block = (sender * NB_DEV + jnp.maximum(send_ids, 0)).astype(jnp.int32).reshape(-1)
    target_block = (receiver * NB_DEV + partner_ids).astype(jnp.int32).reshape(-1)
    velocity = jnp.zeros_like(position)
    for step_index in range(STEPS):
        seg_state = jnp.concatenate([position, line_vec, burgers], axis=1)
        grouped = group_forces(seg_state)
        crossed = cross_forces(seg_state, is_valid, source_block, target_block)
        force = COUPLE * (grouped + crossed) + applied + TENSION * chain_term(position)
        velocity = force / drag_coef[:, None, :]
        speed_sq = lax.optimization_barrier(jnp.sum(velocity * velocity, axis=1))
        time_step = STEP_LENGTH / (jnp.sqrt(jnp.max(speed_sq)) + EPSILON)
        position = position + time_step * velocity
    return (position, velocity)
```

```python
import functools

import jax
import jax.numpy as jnp
from jax import lax
from jax.experimental import pallas as pl
from jax.experimental.pallas import tpu as pltpu
from jax.sharding import PartitionSpec as P

STEPS = 2
COUPLE = 0.0625
CORE_SQUARE = 0.5
TENSION = 0.25
STEP_LENGTH = 1.0
EPSILON = 1e-06

MESH = pl.DeviceIdType.MESH
ROWS = 16
XROW, SROW, PROW = 9, 12, 13
UNROLL_LIMIT = 64


def repeat(first, last, body):
    if last - first <= UNROLL_LIMIT:
        for index in range(first, last):
            body(index)
    else:

        def step(index, carry):
            body(index)
            return carry

        lax.fori_loop(first, last, step, 0)


def kernel(
    n_dom,
    n_sub,
    seg_ref,
    drag_ref,
    stress_ref,
    send_ref,
    partner_ref,
    pos_ref,
    vel_ref,
    stage,
    held,
    numer,
    left_side,
    at_i,
    vel_i,
    acc,
    vel_tx,
    vel_rx,
    top1_tx,
    top1_rx,
    top2_tx,
    top2_rx,
    state_send,
    state_recv,
    vel_send,
    vel_recv,
    top1_send,
    top1_recv,
    top2_send,
    top2_recv,
):
    nb, _, width = seg_ref.shape
    slots = n_sub + n_dom - 1
    dom = lax.axis_index("dom")
    sub = lax.axis_index("sub")

    def sub_at(k):
        return (dom, lax.rem(sub + k, n_sub))

    def dom_at(k):
        return (lax.rem(dom + k, n_dom), sub)

    barrier = pltpu.get_barrier_semaphore()

    def greet_sub(k):
        pl.semaphore_signal(barrier, inc=1, device_id=sub_at(k), device_id_type=MESH)

    def greet_dom(k):
        pl.semaphore_signal(barrier, inc=1, device_id=dom_at(k), device_id_type=MESH)

    repeat(1, n_sub, greet_sub)
    repeat(1, n_dom, greet_dom)

    products = []
    for r in range(nb):
        burgers = seg_ref[r, 6:9, :]
        rows = [burgers[a : a + 1] * seg_ref[r, 3:6, :] for a in range(3)]
        block = jnp.concatenate(rows + [jnp.zeros((ROWS - 9, width), jnp.float32)], axis=0)
        products.append(block)
        held[0, r] = block
        held[0, r, XROW : XROW + 3, :] = seg_ref[r, 0:3, :]

    whole = [held[0, r] for r in range(nb)]
    row_id = lax.broadcasted_iota(jnp.int32, (ROWS, width), 0)

    def fill(q):
        sent = send_ref[0, q].astype(jnp.float32)
        partner = partner_ref[0, q].astype(jnp.float32)
        for r in range(nb):
            stage[q, r] = jnp.where(row_id == SROW, sent, jnp.where(row_id == PROW, partner, whole[r]))

    repeat(0, n_dom, fill)

    def sub_copy(k):
        return pltpu.make_async_remote_copy(
            src_ref=held.at[0],
            dst_ref=held.at[k],
            send_sem=state_send.at[k],
            recv_sem=state_recv.at[k],
            device_id=sub_at(k),
            device_id_type=MESH,
        )

    def dom_copy(k):
        slot = n_sub - 1 + k
        return pltpu.make_async_remote_copy(
            src_ref=stage.at[lax.rem(dom + k, n_dom)],
            dst_ref=held.at[slot],
            send_sem=state_send.at[slot],
            recv_sem=state_recv.at[slot],
            device_id=dom_at(k),
            device_id_type=MESH,
        )

    pl.semaphore_wait(barrier, slots - 1)
    repeat(1, n_dom, lambda k: dom_copy(k).start())
    repeat(1, n_sub, lambda k: sub_copy(k).start())

    applied_rows = []
    drag_rows = []
    for o in range(nb):
        b = [seg_ref[o, 6 + c : 7 + c, :] for c in range(3)]
        ln = [seg_ref[o, 3 + c : 4 + c, :] for c in range(3)]
        pulled = [
            stress_ref[c, 0] * b[0] + stress_ref[c, 1] * b[1] + stress_ref[c, 2] * b[2] for c in range(3)
        ]
        applied_rows.append(pulled[1] * ln[2] - pulled[2] * ln[1])
        applied_rows.append(pulled[2] * ln[0] - pulled[0] * ln[2])
        applied_rows.append(pulled[0] * ln[1] - pulled[1] * ln[0])
        drag_rows.extend([drag_ref[o : o + 1, :]] * 3)
    spare = 8 - 3 * nb
    zeros = jnp.zeros((spare, width), jnp.float32)
    applied = jnp.concatenate(applied_rows + [zeros], axis=0)
    drag = jnp.concatenate(drag_rows + [zeros + 1.0], axis=0)
    position = jnp.concatenate([seg_ref[o, 0:3, :] for o in range(nb)] + [zeros], axis=0)
    lane = lax.broadcasted_iota(jnp.int32, (8, width), 1)

    def split(value):
        high = value.astype(jnp.bfloat16)
        low = (value - high.astype(jnp.float32)).astype(jnp.bfloat16)
        return high, low

    for o in range(nb):
        high = products[o].astype(jnp.bfloat16).astype(jnp.float32)
        low = products[o] - high
        left_side[o] = jnp.concatenate([high, high, low], axis=0).T.astype(jnp.bfloat16)
        turned = whole[o].T
        for c in range(3):
            at_i[o, c] = jnp.broadcast_to(turned[:, XROW + c : XROW + c + 1], (width, width))

    def counts(slot, base, peer):
        table = []
        for o in range(nb):
            row = []
            for r in range(nb):
                value = jnp.full((1, width), base, jnp.float32)
                if peer is not None:
                    sent, partner = send_ref[0, peer], partner_ref[0, peer]
                    mine = jnp.logical_and(sent == o, partner == r)
                    value = value + jnp.where(mine, 1.0, 0.0)
                    source = stage if slot is None else held
                    place = dom if slot is None else slot
                    got, for_mine = source[place, 0, SROW : SROW + 1, :], source[place, 0, PROW : PROW + 1, :]
                    value = value + jnp.where(
                        jnp.logical_and(got == float(r), for_mine == float(o)), 1.0, 0.0
                    )
                row.append(value)
            table.append(row)
        return table

    def fill_numer(slot, base, peer):
        where = 0 if slot is None else slot
        table = counts(slot, base, peer)
        for o in range(nb):
            right = jnp.concatenate([held[where, r] * table[o][r] for r in range(nb)], axis=1)
            high, low = split(right)
            numer[where, o] = jnp.dot(
                left_side[o],
                jnp.concatenate([high, low, high], axis=0),
                preferred_element_type=jnp.float32,
            )

    def add_slot(slot, step, first=False):
        rows = []
        for r in range(nb):
            for c in range(3):
                row = held[slot, r, XROW + c : XROW + c + 1, :]
                if step is not None:
                    row = row + step * vel_rx[slot, r * 3 + c : r * 3 + c + 1, :]
                rows.append(jnp.broadcast_to(row, (8, width)))
        for o in range(nb):
            for g in range(width // 8):
                part = pl.ds(8 * g, 8)
                mine = [at_i[o, c, part, :] for c in range(3)]
                total = None if first else [acc[o, c, part, :] for c in range(3)]
                for r in range(nb):
                    off = [mine[c] - rows[r * 3 + c] for c in range(3)]
                    square = CORE_SQUARE + off[0] * off[0] + off[1] * off[1] + off[2] * off[2]
                    inverse = lax.rsqrt(square)
                    weight = numer[slot, o, part, pl.ds(width * r, width)] * inverse * (inverse * inverse)
                    terms = [weight * off[c] for c in range(3)]
                    total = terms if total is None else [total[c] + terms[c] for c in range(3)]
                for c in range(3):
                    acc[o, c, part, :] = total[c]

    def velocity_of(position):
        sums = []
        for o in range(nb):
            for c in range(3):
                sums.append(jnp.sum(acc[o, c].T, axis=0, keepdims=True))
        pair = jnp.concatenate(sums + [zeros], axis=0)
        before = jnp.where(lane == 0, position, pltpu.roll(position, 1, 1))
        after = jnp.where(lane == width - 1, position, pltpu.roll(position, width - 1, 1))
        chain = before + after - 2.0 * position
        force = COUPLE * pair + applied + TENSION * chain
        velocity = force / drag
        square = velocity * velocity
        tops = []
        for o in range(nb):
            tops.append(square[3 * o : 3 * o + 1] + square[3 * o + 1 : 3 * o + 2] + square[3 * o + 2 : 3 * o + 3])
        return velocity, functools.reduce(jnp.maximum, tops)

    def step_length(row):
        top = jnp.max(row, axis=1, keepdims=True)
        return STEP_LENGTH / (jnp.sqrt(top) + EPSILON)

    fill_numer(None, 1.0, dom)
    add_slot(0, None, first=True)

    def from_sub(k, carry):
        sub_copy(k).wait_recv()
        fill_numer(k, 1.0, None)
        add_slot(k, None)
        return carry

    def from_dom(k, carry):
        slot = n_sub - 1 + k
        dom_copy(k).wait_recv()
        fill_numer(slot, 0.0, lax.rem(dom - k + n_dom, n_dom))
        add_slot(slot, None)
        return carry

    lax.fori_loop(1, n_sub, from_sub, 0)
    lax.fori_loop(1, n_dom, from_dom, 0)
    velocity, top = velocity_of(position)
    vel_tx[...] = jnp.concatenate([velocity[0 : 3 * nb], top, zeros[: spare - 1]], axis=0)
    top1_tx[...] = top

    def vel_copy(slot, target):
        return pltpu.make_async_remote_copy(
            src_ref=vel_tx,
            dst_ref=vel_rx.at[slot],
            send_sem=vel_send,
            recv_sem=vel_recv,
            device_id=target,
            device_id_type=MESH,
        )

    def top1_copy(index):
        kd, ks = index // (n_sub - 1) + 1, index % (n_sub - 1) + 1
        return pltpu.make_async_remote_copy(
            src_ref=top1_tx,
            dst_ref=top1_rx.at[index],
            send_sem=top1_send,
            recv_sem=top1_recv,
            device_id=(lax.rem(dom + kd, n_dom), lax.rem(sub + ks, n_sub)),
            device_id_type=MESH,
        )

    others = (n_sub - 1) * (n_dom - 1)
    repeat(1, n_dom, lambda k: vel_copy(n_sub - 1 + k, dom_at(k)).start())
    repeat(0, others, lambda k: top1_copy(k).start())
    repeat(1, n_sub, lambda k: vel_copy(k, sub_at(k)).start())

    vel_rx[0] = vel_tx[...]
    turned = velocity.T
    for o in range(nb):
        for c in range(3):
            vel_i[o, c] = jnp.broadcast_to(turned[:, 3 * o + c : 3 * o + c + 1], (width, width))

    arrived = vel_rx.at[pl.ds(1, slots - 1)]
    pltpu.make_async_copy(arrived, arrived, vel_recv).wait()
    pltpu.make_async_copy(top1_rx, top1_rx, top1_recv).wait()
    near = jnp.max(vel_rx[:, 3 * nb : 3 * nb + 1, :], axis=0)
    far = jnp.max(top1_rx[...], axis=0)
    step = step_length(jnp.maximum(near, far))

    position = position + step * velocity
    for o in range(nb):
        for c in range(3):
            at_i[o, c] = at_i[o, c] + step * vel_i[o, c]
    add_slot(0, step, first=True)

    def again(slot, carry):
        add_slot(slot, carry)
        return carry

    lax.fori_loop(1, slots, again, step)
    velocity, top = velocity_of(position)
    top2_tx[...] = top

    def top2_copy(index):
        kd, ks = (index + 1) // n_sub, (index + 1) % n_sub
        return pltpu.make_async_remote_copy(
            src_ref=top2_tx,
            dst_ref=top2_rx.at[index],
            send_sem=top2_send,
            recv_sem=top2_recv,
            device_id=(lax.rem(dom + kd, n_dom), lax.rem(sub + ks, n_sub)),
            device_id_type=MESH,
        )

    repeat(0, n_sub * n_dom - 1, lambda k: top2_copy(k).start())
    for o in range(nb):
        vel_ref[o] = velocity[3 * o : 3 * o + 3]

    repeat(1, n_sub, lambda k: sub_copy(k).wait_send())
    repeat(1, n_dom, lambda k: dom_copy(k).wait_send())
    pltpu.make_async_copy(arrived, arrived, vel_send).wait()
    pltpu.make_async_copy(top1_rx, top1_rx, top1_send).wait()

    pltpu.make_async_copy(top2_rx, top2_rx, top2_recv).wait()
    step = step_length(jnp.maximum(jnp.max(top2_rx[...], axis=0), top))
    position = position + step * velocity
    for o in range(nb):
        pos_ref[o] = position[3 * o : 3 * o + 3]
    pltpu.make_async_copy(top2_rx, top2_rx, top2_send).wait()


def solution(mesh):
    n_dom, n_sub = mesh.shape["dom"], mesh.shape["sub"]

    def local(segments, stress, drag_coef, send_ids, partner_ids):
        nb, _, width = segments.shape
        slots = n_sub + n_dom - 1
        f32 = jnp.float32
        vmem = pl.BlockSpec(memory_space=pltpu.VMEM)
        smem = pl.BlockSpec(memory_space=pltpu.SMEM)
        out = jax.ShapeDtypeStruct((nb, 3, width), f32)
        words = slots * nb * width * nb * width + (n_dom + slots) * nb * ROWS * width + 9 * nb * width * width
        return pl.pallas_call(
            functools.partial(kernel, n_dom, n_sub),
            out_shape=(out, out),
            in_specs=[vmem, vmem, smem, smem, smem],
            out_specs=(vmem, vmem),
            scratch_shapes=[
                pltpu.VMEM((n_dom, nb, ROWS, width), f32),
                pltpu.VMEM((slots, nb, ROWS, width), f32),
                pltpu.VMEM((slots, nb, width, nb * width), f32),
                pltpu.VMEM((nb, width, 3 * ROWS), jnp.bfloat16),
                pltpu.VMEM((nb, 3, width, width), f32),
                pltpu.VMEM((nb, 3, width, width), f32),
                pltpu.VMEM((nb, 3, width, width), f32),
                pltpu.VMEM((8, width), f32),
                pltpu.VMEM((slots, 8, width), f32),
                pltpu.VMEM((1, width), f32),
                pltpu.VMEM(((n_dom - 1) * (n_sub - 1), 1, width), f32),
                pltpu.VMEM((1, width), f32),
                pltpu.VMEM((n_dom * n_sub - 1, 1, width), f32),
                pltpu.SemaphoreType.DMA((slots,)),
                pltpu.SemaphoreType.DMA((slots,)),
                pltpu.SemaphoreType.DMA,
                pltpu.SemaphoreType.DMA,
                pltpu.SemaphoreType.DMA,
                pltpu.SemaphoreType.DMA,
                pltpu.SemaphoreType.DMA,
                pltpu.SemaphoreType.DMA,
            ],
            compiler_params=pltpu.CompilerParams(
                collective_id=0,
                has_side_effects=True,
                vmem_limit_bytes=4 * words + 8 * 1024 * 1024,
            ),
        )(
            segments,
            drag_coef,
            stress,
            send_ids.reshape(1, n_dom),
            partner_ids.reshape(1, n_dom),
        )

    in_specs = (
        P(("dom", "sub"), None, None),
        P(),
        P(("dom", "sub"), None),
        P(("dom", "sub"), None, None),
        P(("dom", "sub"), None, None),
    )
    out_specs = (P(("dom", "sub"), None, None), P(("dom", "sub"), None, None))
    return jax.shard_map(local, mesh=mesh, in_specs=in_specs, out_specs=out_specs, check_vma=False)
```

```python
import functools

import jax
import jax.numpy as jnp
from jax import lax
from jax.experimental import pallas as pl
from jax.experimental.pallas import tpu as pltpu
from jax.sharding import PartitionSpec as P

STEPS = 2
COUPLE = 0.0625
CORE_SQUARE = 0.5
TENSION = 0.25
STEP_LENGTH = 1.0
EPSILON = 1e-06

MESH = pl.DeviceIdType.MESH
ROWS = 16
UNROLL_LIMIT = 64


def repeat(first, last, body):
    if last - first <= UNROLL_LIMIT:
        for index in range(first, last):
            body(index)
    else:

        def step(index, carry):
            body(index)
            return carry

        lax.fori_loop(first, last, step, 0)


def kernel(
    n_dom,
    n_sub,
    seg_ref,
    drag_ref,
    stress_ref,
    send_ref,
    partner_ref,
    pos_ref,
    vel_ref,
    stage,
    held,
    numer,
    left_side,
    at_i,
    vel_i,
    acc,
    row_sum,
    moved,
    applied_ref,
    drag8_ref,
    vel_tx,
    vel_rx,
    top1_tx,
    top1_rx,
    top2_tx,
    top2_rx,
    state_send,
    state_recv,
    vel_send,
    vel_recv,
    top1_send,
    top1_recv,
    top2_send,
    top2_recv,
):
    _, nb, width = seg_ref.shape
    slots = n_sub + n_dom - 1
    dom = lax.axis_index("dom")
    sub = lax.axis_index("sub")
    used = 3 * nb
    tail = nb * ROWS

    if n_dom <= UNROLL_LIMIT:
        dom_ids = [lax.rem(dom + k, n_dom) for k in range(n_dom)]
    sub_ids = [lax.rem(sub + k, n_sub) for k in range(n_sub)]

    def dom_id(k):
        return dom_ids[k] if isinstance(k, int) else lax.rem(dom + k, n_dom)

    def sub_id(k):
        return sub_ids[k] if isinstance(k, int) else lax.rem(sub + k, n_sub)

    barrier = pltpu.get_barrier_semaphore()

    def greet(dom_to, sub_to):
        pl.semaphore_signal(barrier, inc=1, device_id=(dom_to, sub_to), device_id_type=MESH)

    repeat(1, n_dom, lambda k: greet(dom_id(k), sub))
    repeat(1, n_sub, lambda k: greet(dom, sub_id(k)))

    held[0] = jnp.zeros((tail + 8, width), jnp.float32)
    for a in range(3):
        for c in range(3):
            product = seg_ref[6 + a] * seg_ref[3 + c]
            for r in range(nb):
                held[0, ROWS * r + 3 * a + c] = product[r]
    for c in range(3):
        for r in range(nb):
            held[0, tail + 3 * r + c] = seg_ref[c, r]
    products = [held[0, ROWS * r : ROWS * (r + 1), :] for r in range(nb)]
    position = held[0, tail : tail + 8, :]
    row_id = lax.broadcasted_iota(jnp.int32, (8, width), 0)
    lane = lax.broadcasted_iota(jnp.int32, (8, width), 1)

    def fill(q):
        sent = send_ref[0, q].astype(jnp.float32)
        partner = partner_ref[0, q].astype(jnp.float32)
        for r in range(nb):
            stage[q, ROWS * r : ROWS * (r + 1), :] = products[r]
        entries = jnp.where(row_id == used, sent, jnp.where(row_id == used + 1, partner, position))
        stage[q, tail : tail + 8, :] = entries

    repeat(0, n_dom, fill)

    def sub_copy(k):
        return pltpu.make_async_remote_copy(
            src_ref=held.at[0],
            dst_ref=held.at[k],
            send_sem=state_send.at[k],
            recv_sem=state_recv.at[k],
            device_id=(dom, sub_id(k)),
            device_id_type=MESH,
        )

    def dom_copy(k):
        slot = n_sub - 1 + k
        return pltpu.make_async_remote_copy(
            src_ref=stage.at[dom_id(k)],
            dst_ref=held.at[slot],
            send_sem=state_send.at[slot],
            recv_sem=state_recv.at[slot],
            device_id=(dom_id(k), sub),
            device_id_type=MESH,
        )

    pl.semaphore_wait(barrier, slots - 1)
    repeat(1, n_dom, lambda k: dom_copy(k).start())
    repeat(1, n_sub, lambda k: sub_copy(k).start())

    b = [seg_ref[6 + c] for c in range(3)]
    ln = [seg_ref[3 + c] for c in range(3)]
    pulled = [
        stress_ref[c, 0] * b[0] + stress_ref[c, 1] * b[1] + stress_ref[c, 2] * b[2] for c in range(3)
    ]
    crossed = [
        pulled[1] * ln[2] - pulled[2] * ln[1],
        pulled[2] * ln[0] - pulled[0] * ln[2],
        pulled[0] * ln[1] - pulled[1] * ln[0],
    ]
    applied_ref[...] = jnp.zeros((8, width), jnp.float32)
    drag8_ref[...] = jnp.ones((8, width), jnp.float32)
    for o in range(nb):
        for c in range(3):
            applied_ref[3 * o + c] = crossed[c][o]
            drag8_ref[3 * o + c] = drag_ref[o]

    def split(value):
        high = value.astype(jnp.bfloat16)
        low = (value - high.astype(jnp.float32)).astype(jnp.bfloat16)
        return high, low

    def spread(target, tile):
        turned = tile.T
        for row in range(used):
            target[row] = jnp.broadcast_to(turned[:, row : row + 1], (width, width))

    spread(at_i, position)
    for o in range(nb):
        high = products[o].astype(jnp.bfloat16).astype(jnp.float32)
        low = products[o] - high
        left_side[o] = jnp.concatenate([high, high, low], axis=0).T.astype(jnp.bfloat16)

    def counts(base, peer, entries):
        table = []
        for o in range(nb):
            row = []
            for r in range(nb):
                value = jnp.full((1, width), base, jnp.float32)
                if peer is not None:
                    mine = jnp.logical_and(send_ref[0, peer] == o, partner_ref[0, peer] == r)
                    got, for_mine = entries
                    theirs = jnp.logical_and(got == float(r), for_mine == float(o))
                    value = value + jnp.where(mine, 1.0, 0.0) + jnp.where(theirs, 1.0, 0.0)
                row.append(value)
            table.append(row)
        return table

    def fill_numer(slot, base, peer, source=None, place=None):
        entries = None
        if peer is not None:
            entries = [source[place, tail + used + e : tail + used + e + 1, :] for e in range(2)]
        table = counts(base, peer, entries)
        for o in range(nb):
            pieces = [held[slot, ROWS * r : ROWS * (r + 1), :] * table[o][r] for r in range(nb)]
            high, low = split(jnp.concatenate(pieces, axis=1))
            numer[slot, o] = jnp.dot(
                left_side[o],
                jnp.concatenate([high, low, high], axis=0),
                preferred_element_type=jnp.float32,
            )

    def add_slots(members, source, first_row, first, last, step=None):
        def chunk(g, carry):
            part = pl.ds(pl.multiple_of(8 * g, 8), 8)
            mine = [at_i[row, part, :] for row in range(used)]
            if step is not None:
                mine = [mine[row] + step * vel_i[row, part, :] for row in range(used)]
            total = [None if first else acc[row, part, :] for row in range(used)]

            def add_one(slot, total):
                total = list(total)
                for r in range(nb):
                    theirs = [
                        jnp.broadcast_to(source[slot, pl.ds(first_row + 3 * r + c, 1), :], (8, width))
                        for c in range(3)
                    ]
                    for o in range(nb):
                        off = [mine[3 * o + c] - theirs[c] for c in range(3)]
                        square = CORE_SQUARE + off[0] * off[0] + off[1] * off[1] + off[2] * off[2]
                        inverse = lax.rsqrt(square)
                        weight = numer[slot, o, part, pl.ds(width * r, width)] * inverse * (inverse * inverse)
                        for c in range(3):
                            term = weight * off[c]
                            row = 3 * o + c
                            total[row] = term if total[row] is None else total[row] + term
                return total

            if members[1] - members[0] <= UNROLL_LIMIT:
                for slot in range(*members):
                    total = add_one(slot, total)
            else:
                if first:
                    total = [jnp.zeros((8, width), jnp.float32)] * used
                total = lax.fori_loop(members[0], members[1], add_one, total)
            if last:
                tile = jnp.zeros((8, width), jnp.float32)
                for row in range(used):
                    tile = jnp.where(lane == row, jnp.sum(total[row], axis=1, keepdims=True), tile)
                row_sum[part, :] = tile
            else:
                for row in range(used):
                    acc[row, part, :] = total[row]
            return carry

        lax.fori_loop(0, width // 8, chunk, 0)

    def velocity_of(position):
        pair = row_sum[...].T[0:8]
        before = jnp.where(lane == 0, position, pltpu.roll(position, 1, 1))
        after = jnp.where(lane == width - 1, position, pltpu.roll(position, width - 1, 1))
        chain = before + after - 2.0 * position
        force = COUPLE * pair + applied_ref[...] + TENSION * chain
        velocity = force / drag8_ref[...]
        square = velocity * velocity
        tops = []
        for o in range(nb):
            tops.append(square[3 * o : 3 * o + 1] + square[3 * o + 1 : 3 * o + 2] + square[3 * o + 2 : 3 * o + 3])
        return velocity, functools.reduce(jnp.maximum, tops)

    def step_length(row):
        top = jnp.max(row, axis=1, keepdims=True)
        return STEP_LENGTH / (jnp.sqrt(top) + EPSILON)

    fill_numer(0, 1.0, dom, stage, dom)
    add_slots((0, 1), held, tail, True, False)

    def from_sub(k, carry):
        sub_copy(k).wait_recv()
        fill_numer(k, 1.0, None)
        return carry

    def from_dom(k, carry):
        slot = n_sub - 1 + k
        dom_copy(k).wait_recv()
        fill_numer(slot, 0.0, lax.rem(dom - k + n_dom, n_dom), held, slot)
        return carry

    lax.fori_loop(1, n_sub, from_sub, 0)
    add_slots((1, n_sub), held, tail, False, False)
    lax.fori_loop(1, n_dom, from_dom, 0)
    add_slots((n_sub, slots), held, tail, False, True)
    velocity, top = velocity_of(position)
    vel_tx[...] = jnp.where(row_id == used, top, velocity)
    top1_tx[...] = top

    def vel_copy(slot, dom_to, sub_to):
        return pltpu.make_async_remote_copy(
            src_ref=vel_tx,
            dst_ref=vel_rx.at[slot],
            send_sem=vel_send,
            recv_sem=vel_recv,
            device_id=(dom_to, sub_to),
            device_id_type=MESH,
        )

    def top1_copy(index):
        kd, ks = index // (n_sub - 1) + 1, index % (n_sub - 1) + 1
        return pltpu.make_async_remote_copy(
            src_ref=top1_tx,
            dst_ref=top1_rx.at[index],
            send_sem=top1_send,
            recv_sem=top1_recv,
            device_id=(dom_id(kd), sub_id(ks)),
            device_id_type=MESH,
        )

    others = (n_sub - 1) * (n_dom - 1)
    repeat(1, n_dom, lambda k: vel_copy(n_sub - 1 + k, dom_id(k), sub).start())
    repeat(0, others, lambda k: top1_copy(k).start())
    repeat(1, n_sub, lambda k: vel_copy(k, dom, sub_id(k)).start())

    vel_rx[0] = vel_tx[...]
    spread(vel_i, velocity)

    arrived = vel_rx.at[pl.ds(1, slots - 1)]
    pltpu.make_async_copy(arrived, arrived, vel_recv).wait()
    pltpu.make_async_copy(top1_rx, top1_rx, top1_recv).wait()
    near = jnp.max(vel_rx[...], axis=0)[used : used + 1]
    far = jnp.max(top1_rx[...], axis=0)
    step = step_length(jnp.maximum(near, far))

    position = position + step * velocity

    def move(slot):
        moved[slot] = held[slot, tail : tail + 8, :] + step * vel_rx[slot]

    repeat(0, slots, move)
    add_slots((0, slots), moved, 0, True, True, step)
    velocity, top = velocity_of(position)
    top2_tx[...] = top

    def top2_copy(index):
        kd, ks = (index + 1) // n_sub, (index + 1) % n_sub
        return pltpu.make_async_remote_copy(
            src_ref=top2_tx,
            dst_ref=top2_rx.at[index],
            send_sem=top2_send,
            recv_sem=top2_recv,
            device_id=(dom_id(kd), sub_id(ks)),
            device_id_type=MESH,
        )

    repeat(0, n_sub * n_dom - 1, lambda k: top2_copy(k).start())
    for o in range(nb):
        for c in range(3):
            vel_ref[c, o] = velocity[3 * o + c]

    repeat(1, n_sub, lambda k: sub_copy(k).wait_send())
    repeat(1, n_dom, lambda k: dom_copy(k).wait_send())
    pltpu.make_async_copy(arrived, arrived, vel_send).wait()
    pltpu.make_async_copy(top1_rx, top1_rx, top1_send).wait()

    pltpu.make_async_copy(top2_rx, top2_rx, top2_recv).wait()
    step = step_length(jnp.maximum(jnp.max(top2_rx[...], axis=0), top))
    position = position + step * velocity
    for o in range(nb):
        for c in range(3):
            pos_ref[c, o] = position[3 * o + c]
    pltpu.make_async_copy(top2_rx, top2_rx, top2_send).wait()


def solution(mesh):
    n_dom, n_sub = mesh.shape["dom"], mesh.shape["sub"]

    def local(segments, stress, drag_coef, send_ids, partner_ids):
        nb, _, width = segments.shape
        slots = n_sub + n_dom - 1
        rows = nb * ROWS + 8
        f32 = jnp.float32
        vmem = pl.BlockSpec(memory_space=pltpu.VMEM)
        smem = pl.BlockSpec(memory_space=pltpu.SMEM)
        out = jax.ShapeDtypeStruct((3, nb, width), f32)
        words = slots * nb * width * nb * width + (n_dom + slots) * rows * width + 10 * nb * width * width
        words += 16 * slots * width
        dma = pltpu.SemaphoreType.DMA
        position, velocity = pl.pallas_call(
            functools.partial(kernel, n_dom, n_sub),
            out_shape=(out, out),
            in_specs=[vmem, vmem, smem, smem, smem],
            out_specs=(vmem, vmem),
            scratch_shapes=[
                pltpu.VMEM((n_dom, rows, width), f32),
                pltpu.VMEM((slots, rows, width), f32),
                pltpu.VMEM((slots, nb, width, nb * width), f32),
                pltpu.VMEM((nb, width, 3 * ROWS), jnp.bfloat16),
                pltpu.VMEM((3 * nb, width, width), f32),
                pltpu.VMEM((3 * nb, width, width), f32),
                pltpu.VMEM((3 * nb, width, width), f32),
                pltpu.VMEM((width, width), f32),
                pltpu.VMEM((slots, 8, width), f32),
                pltpu.VMEM((8, width), f32),
                pltpu.VMEM((8, width), f32),
                pltpu.VMEM((8, width), f32),
                pltpu.VMEM((slots, 8, width), f32),
                pltpu.VMEM((1, width), f32),
                pltpu.VMEM(((n_dom - 1) * (n_sub - 1), 1, width), f32),
                pltpu.VMEM((1, width), f32),
                pltpu.VMEM((n_dom * n_sub - 1, 1, width), f32),
                dma((slots,)),
                dma((slots,)),
                dma,
                dma,
                dma,
                dma,
                dma,
                dma,
            ],
            compiler_params=pltpu.CompilerParams(
                collective_id=0,
                has_side_effects=True,
                vmem_limit_bytes=4 * words + 8 * 1024 * 1024,
            ),
        )(
            segments.transpose(1, 0, 2),
            drag_coef,
            stress,
            send_ids.reshape(1, n_dom),
            partner_ids.reshape(1, n_dom),
        )
        return position.transpose(1, 0, 2), velocity.transpose(1, 0, 2)

    in_specs = (
        P(("dom", "sub"), None, None),
        P(),
        P(("dom", "sub"), None),
        P(("dom", "sub"), None, None),
        P(("dom", "sub"), None, None),
    )
    out_specs = (P(("dom", "sub"), None, None), P(("dom", "sub"), None, None))
    return jax.shard_map(local, mesh=mesh, in_specs=in_specs, out_specs=out_specs, check_vma=False)
```

```python
import functools

import jax
import jax.numpy as jnp
from jax import lax
from jax.experimental import pallas as pl
from jax.experimental.pallas import tpu as pltpu
from jax.sharding import PartitionSpec as P

STEPS = 2
COUPLE = 0.0625
CORE_SQUARE = 0.5
TENSION = 0.25
STEP_LENGTH = 1.0
EPSILON = 1e-06

MESH = pl.DeviceIdType.MESH
ROWS = 16
UNROLL_LIMIT = 64


def repeat(first, last, body):
    if last - first <= UNROLL_LIMIT:
        for index in range(first, last):
            body(index)
    else:

        def step(index, carry):
            body(index)
            return carry

        lax.fori_loop(first, last, step, 0)


def kernel(
    n_dom,
    n_sub,
    seg_ref,
    drag_ref,
    stress_ref,
    send_ref,
    partner_ref,
    pos_ref,
    vel_ref,
    top_ref,
    stage,
    held,
    numer,
    left_side,
    at_i,
    vel_i,
    acc,
    sources,
    applied_ref,
    drag8_ref,
    vel_tx,
    vel_rx,
    top1_tx,
    top1_rx,
    top2_tx,
    top2_rx,
    state_send,
    state_recv,
    vel_send,
    vel_recv,
    top1_send,
    top1_recv,
    top2_send,
    top2_recv,
):
    nb, _, width = seg_ref.shape
    slots = n_sub + n_dom - 1
    dom = lax.axis_index("dom")
    sub = lax.axis_index("sub")
    used = 3 * nb
    tail = nb * ROWS

    if n_dom <= UNROLL_LIMIT:
        dom_ids = [lax.rem(dom + k, n_dom) for k in range(n_dom)]
    sub_ids = [lax.rem(sub + k, n_sub) for k in range(n_sub)]

    def dom_id(k):
        return dom_ids[k] if isinstance(k, int) else lax.rem(dom + k, n_dom)

    def sub_id(k):
        return sub_ids[k] if isinstance(k, int) else lax.rem(sub + k, n_sub)

    barrier = pltpu.get_barrier_semaphore()

    def greet(dom_to, sub_to):
        pl.semaphore_signal(barrier, inc=1, device_id=(dom_to, sub_to), device_id_type=MESH)

    repeat(1, n_dom, lambda k: greet(dom_id(k), sub))
    repeat(1, n_sub, lambda k: greet(dom, sub_id(k)))

    held[0] = jnp.zeros((tail + 8, width), jnp.float32)
    for r in range(nb):
        for a in range(3):
            held[0, ROWS * r + 3 * a : ROWS * r + 3 * a + 3, :] = seg_ref[r, 6 + a : 7 + a, :] * seg_ref[r, 3:6, :]
        held[0, tail + 3 * r : tail + 3 * r + 3, :] = seg_ref[r, 0:3, :]
    products = [held[0, ROWS * r : ROWS * (r + 1), :] for r in range(nb)]
    position = held[0, tail : tail + 8, :]
    row_id = lax.broadcasted_iota(jnp.int32, (8, width), 0)
    lane = lax.broadcasted_iota(jnp.int32, (8, width), 1)

    def fill(q):
        sent = send_ref[0, q].astype(jnp.float32)
        partner = partner_ref[0, q].astype(jnp.float32)
        for r in range(nb):
            stage[q, ROWS * r : ROWS * (r + 1), :] = products[r]
        entries = jnp.where(row_id == used, sent, jnp.where(row_id == used + 1, partner, position))
        stage[q, tail : tail + 8, :] = entries

    repeat(0, n_dom, fill)

    def sub_copy(k):
        return pltpu.make_async_remote_copy(
            src_ref=held.at[0],
            dst_ref=held.at[k],
            send_sem=state_send.at[k],
            recv_sem=state_recv.at[k],
            device_id=(dom, sub_id(k)),
            device_id_type=MESH,
        )

    def dom_copy(k):
        slot = n_sub - 1 + k
        return pltpu.make_async_remote_copy(
            src_ref=stage.at[dom_id(k)],
            dst_ref=held.at[slot],
            send_sem=state_send.at[slot],
            recv_sem=state_recv.at[slot],
            device_id=(dom_id(k), sub),
            device_id_type=MESH,
        )

    pl.semaphore_wait(barrier, slots - 1)
    repeat(1, n_dom, lambda k: dom_copy(k).start())
    repeat(1, n_sub, lambda k: sub_copy(k).start())

    applied_ref[...] = jnp.zeros((8, width), jnp.float32)
    drag8_ref[...] = jnp.ones((8, width), jnp.float32)
    for o in range(nb):
        b = [seg_ref[o, 6 + c : 7 + c, :] for c in range(3)]
        ln = [seg_ref[o, 3 + c : 4 + c, :] for c in range(3)]
        pulled = [
            stress_ref[c, 0] * b[0] + stress_ref[c, 1] * b[1] + stress_ref[c, 2] * b[2] for c in range(3)
        ]
        applied_ref[3 * o : 3 * o + 1, :] = pulled[1] * ln[2] - pulled[2] * ln[1]
        applied_ref[3 * o + 1 : 3 * o + 2, :] = pulled[2] * ln[0] - pulled[0] * ln[2]
        applied_ref[3 * o + 2 : 3 * o + 3, :] = pulled[0] * ln[1] - pulled[1] * ln[0]
        for c in range(3):
            drag8_ref[3 * o + c : 3 * o + c + 1, :] = drag_ref[o : o + 1, :]

    def split(value):
        high = value.astype(jnp.bfloat16)
        low = (value - high.astype(jnp.float32)).astype(jnp.bfloat16)
        return high, low

    def spread(target, tile):
        turned = tile.T
        for row in range(used):
            target[row] = jnp.broadcast_to(turned[:, row : row + 1], (width, width))

    spread(at_i, position)
    for o in range(nb):
        high = products[o].astype(jnp.bfloat16).astype(jnp.float32)
        low = products[o] - high
        left_side[o] = jnp.concatenate([high, high, low], axis=0).T.astype(jnp.bfloat16)

    def counts(base, peer, entries):
        table = []
        for o in range(nb):
            row = []
            for r in range(nb):
                value = jnp.full((1, width), base, jnp.float32)
                if peer is not None:
                    mine = jnp.logical_and(send_ref[0, peer] == o, partner_ref[0, peer] == r)
                    got, for_mine = entries
                    theirs = jnp.logical_and(got == float(r), for_mine == float(o))
                    value = value + jnp.where(mine, 1.0, 0.0) + jnp.where(theirs, 1.0, 0.0)
                row.append(value)
            table.append(row)
        return table

    def fill_numer(slot, base, peer, source=None, place=None):
        entries = None
        if peer is not None:
            entries = [source[place, tail + used + e : tail + used + e + 1, :] for e in range(2)]
        table = counts(base, peer, entries)
        for o in range(nb):
            pieces = [held[slot, ROWS * r : ROWS * (r + 1), :] * table[o][r] for r in range(nb)]
            high, low = split(jnp.concatenate(pieces, axis=1))
            numer[slot, o] = jnp.dot(
                left_side[o],
                jnp.concatenate([high, low, high], axis=0),
                preferred_element_type=jnp.float32,
            )

    def spread_sources(slot, tile):
        for row in range(used):
            sources[slot, row] = jnp.broadcast_to(tile[row : row + 1], (8, width))

    def add_slots(members, first, unroll, step=None):
        def chunk(g, carry):
            part = pl.ds(pl.multiple_of(8 * g, 8), 8)
            mine = [at_i[row, part, :] for row in range(used)]
            if step is not None:
                mine = [mine[row] + step * vel_i[row, part, :] for row in range(used)]
            total = [None if first else acc[row, part, :] for row in range(used)]

            def add_one(slot, total):
                total = list(total)
                for r in range(nb):
                    theirs = [sources[slot, 3 * r + c] for c in range(3)]
                    for o in range(nb):
                        off = [mine[3 * o + c] - theirs[c] for c in range(3)]
                        square = CORE_SQUARE + off[0] * off[0] + off[1] * off[1] + off[2] * off[2]
                        inverse = lax.rsqrt(square)
                        weight = numer[slot, o, part, pl.ds(width * r, width)] * inverse * (inverse * inverse)
                        for c in range(3):
                            term = weight * off[c]
                            row = 3 * o + c
                            total[row] = term if total[row] is None else total[row] + term
                return total

            if members[1] - members[0] <= UNROLL_LIMIT:
                for slot in range(*members):
                    total = add_one(slot, total)
            else:
                if first:
                    total = [jnp.zeros((8, width), jnp.float32)] * used
                total = lax.fori_loop(members[0], members[1], add_one, total)
            for row in range(used):
                acc[row, part, :] = total[row]
            return carry

        lax.fori_loop(0, width // 8, chunk, 0, unroll=unroll)

    def velocity_of(position):
        sums = [jnp.sum(acc[row].T, axis=0, keepdims=True) for row in range(used)]
        pair = jnp.concatenate(sums + [jnp.zeros((8 - used, width), jnp.float32)], axis=0)
        before = jnp.where(lane == 0, position, pltpu.roll(position, 1, 1))
        after = jnp.where(lane == width - 1, position, pltpu.roll(position, width - 1, 1))
        chain = before + after - 2.0 * position
        force = COUPLE * pair + applied_ref[...] + TENSION * chain
        velocity = force / drag8_ref[...]
        square = velocity * velocity
        tops = []
        for o in range(nb):
            tops.append(square[3 * o : 3 * o + 1] + square[3 * o + 1 : 3 * o + 2] + square[3 * o + 2 : 3 * o + 3])
        return velocity, functools.reduce(jnp.maximum, tops)

    def step_length(row):
        top = jnp.max(row, axis=1, keepdims=True)
        return STEP_LENGTH / (jnp.sqrt(top) + EPSILON)

    fill_numer(0, 1.0, dom, stage, dom)
    spread_sources(0, position)
    add_slots((0, 1), True, 8)

    def from_sub(k, carry):
        sub_copy(k).wait_recv()
        fill_numer(k, 1.0, None)
        spread_sources(k, held[k, tail : tail + 8, :])
        return carry

    def from_dom(k, carry):
        slot = n_sub - 1 + k
        dom_copy(k).wait_recv()
        fill_numer(slot, 0.0, lax.rem(dom - k + n_dom, n_dom), held, slot)
        spread_sources(slot, held[slot, tail : tail + 8, :])
        return carry

    lax.fori_loop(1, n_sub, from_sub, 0)
    add_slots((1, n_sub), False, 4)
    lax.fori_loop(1, n_dom, from_dom, 0)
    add_slots((n_sub, slots), False, 4)
    velocity, top = velocity_of(position)
    vel_tx[...] = jnp.where(row_id == used, top, velocity)
    top1_tx[...] = top

    def vel_copy(slot, dom_to, sub_to):
        return pltpu.make_async_remote_copy(
            src_ref=vel_tx,
            dst_ref=vel_rx.at[slot],
            send_sem=vel_send,
            recv_sem=vel_recv,
            device_id=(dom_to, sub_to),
            device_id_type=MESH,
        )

    def top1_copy(index):
        kd, ks = index // (n_sub - 1) + 1, index % (n_sub - 1) + 1
        return pltpu.make_async_remote_copy(
            src_ref=top1_tx,
            dst_ref=top1_rx.at[index],
            send_sem=top1_send,
            recv_sem=top1_recv,
            device_id=(dom_id(kd), sub_id(ks)),
            device_id_type=MESH,
        )

    others = (n_sub - 1) * (n_dom - 1)
    repeat(1, n_dom, lambda k: vel_copy(n_sub - 1 + k, dom_id(k), sub).start())
    repeat(0, others, lambda k: top1_copy(k).start())
    repeat(1, n_sub, lambda k: vel_copy(k, dom, sub_id(k)).start())

    vel_rx[0] = vel_tx[...]
    spread(vel_i, velocity)

    arrived = vel_rx.at[pl.ds(1, slots - 1)]
    pltpu.make_async_copy(arrived, arrived, vel_recv).wait()
    pltpu.make_async_copy(top1_rx, top1_rx, top1_recv).wait()
    near = jnp.max(vel_rx[...], axis=0)[used : used + 1]
    far = jnp.max(top1_rx[...], axis=0)
    step = step_length(jnp.maximum(near, far))

    position = position + step * velocity

    def move(slot):
        spread_sources(slot, held[slot, tail : tail + 8, :] + step * vel_rx[slot])

    repeat(0, slots, move)
    add_slots((0, slots), True, 4, step)
    velocity, top = velocity_of(position)
    top2_tx[...] = top

    def top2_copy(index):
        kd, ks = (index + 1) // n_sub, (index + 1) % n_sub
        return pltpu.make_async_remote_copy(
            src_ref=top2_tx,
            dst_ref=top2_rx.at[index],
            send_sem=top2_send,
            recv_sem=top2_recv,
            device_id=(dom_id(kd), sub_id(ks)),
            device_id_type=MESH,
        )

    repeat(0, n_sub * n_dom - 1, lambda k: top2_copy(k).start())
    vel_ref[...] = velocity
    pos_ref[...] = position

    repeat(1, n_sub, lambda k: sub_copy(k).wait_send())
    repeat(1, n_dom, lambda k: dom_copy(k).wait_send())
    pltpu.make_async_copy(arrived, arrived, vel_send).wait()
    pltpu.make_async_copy(top1_rx, top1_rx, top1_send).wait()

    pltpu.make_async_copy(top2_rx, top2_rx, top2_recv).wait()
    top_ref[...] = jnp.maximum(jnp.max(top2_rx[...], axis=0), top)
    pltpu.make_async_copy(top2_rx, top2_rx, top2_send).wait()


def last_move(pos8_ref, vel8_ref, top_ref, pos_ref, vel_ref):
    _, nb, _ = pos_ref.shape
    step = STEP_LENGTH / (jnp.sqrt(jnp.max(top_ref[...], axis=1, keepdims=True)) + EPSILON)
    velocity = vel8_ref[...]
    position = pos8_ref[...] + step * velocity
    for o in range(nb):
        for c in range(3):
            vel_ref[c, o] = velocity[3 * o + c]
            pos_ref[c, o] = position[3 * o + c]


def solution(mesh):
    n_dom, n_sub = mesh.shape["dom"], mesh.shape["sub"]

    def local(segments, stress, drag_coef, send_ids, partner_ids):
        nb, _, width = segments.shape
        slots = n_sub + n_dom - 1
        rows = nb * ROWS + 8
        f32 = jnp.float32
        vmem = pl.BlockSpec(memory_space=pltpu.VMEM)
        out = jax.ShapeDtypeStruct((3, nb, width), f32)
        words = slots * nb * width * nb * width + (n_dom + slots) * rows * width + 10 * nb * width * width
        words += 64 * slots * width
        dma = pltpu.SemaphoreType.DMA
        tile = jax.ShapeDtypeStruct((8, width), f32)
        smem = pl.BlockSpec(memory_space=pltpu.SMEM)
        moved = pl.pallas_call(
            functools.partial(kernel, n_dom, n_sub),
            out_shape=(tile, tile, jax.ShapeDtypeStruct((1, width), f32)),
            in_specs=[vmem, vmem, smem, smem, smem],
            out_specs=(vmem, vmem, vmem),
            scratch_shapes=[
                pltpu.VMEM((n_dom, rows, width), f32),
                pltpu.VMEM((slots, rows, width), f32),
                pltpu.VMEM((slots, nb, width, nb * width), f32),
                pltpu.VMEM((nb, width, 3 * ROWS), jnp.bfloat16),
                pltpu.VMEM((3 * nb, width, width), f32),
                pltpu.VMEM((3 * nb, width, width), f32),
                pltpu.VMEM((3 * nb, width, width), f32),
                pltpu.VMEM((slots, 3 * nb, 8, width), f32),
                pltpu.VMEM((8, width), f32),
                pltpu.VMEM((8, width), f32),
                pltpu.VMEM((8, width), f32),
                pltpu.VMEM((slots, 8, width), f32),
                pltpu.VMEM((1, width), f32),
                pltpu.VMEM(((n_dom - 1) * (n_sub - 1), 1, width), f32),
                pltpu.VMEM((1, width), f32),
                pltpu.VMEM((n_dom * n_sub - 1, 1, width), f32),
                dma((slots,)),
                dma((slots,)),
                dma,
                dma,
                dma,
                dma,
                dma,
                dma,
            ],
            compiler_params=pltpu.CompilerParams(
                collective_id=0,
                has_side_effects=True,
                vmem_limit_bytes=4 * words + 8 * 1024 * 1024,
            ),
        )(
            segments,
            drag_coef,
            stress,
            send_ids.reshape(1, n_dom),
            partner_ids.reshape(1, n_dom),
        )
        position, velocity = pl.pallas_call(
            last_move,
            out_shape=(out, out),
            in_specs=[vmem, vmem, vmem],
            out_specs=(vmem, vmem),
        )(*moved)
        return position.transpose(1, 0, 2), velocity.transpose(1, 0, 2)

    in_specs = (
        P(("dom", "sub"), None, None),
        P(),
        P(("dom", "sub"), None),
        P(("dom", "sub"), None, None),
        P(("dom", "sub"), None, None),
    )
    out_specs = (P(("dom", "sub"), None, None), P(("dom", "sub"), None, None))
    return jax.shard_map(local, mesh=mesh, in_specs=in_specs, out_specs=out_specs, check_vma=False)
```

```python
import functools

import jax
import jax.numpy as jnp
from jax import lax
from jax.experimental import pallas as pl
from jax.experimental.pallas import tpu as pltpu
from jax.sharding import PartitionSpec as P

STEPS = 2
COUPLE = 0.0625
CORE_SQUARE = 0.5
TENSION = 0.25
STEP_LENGTH = 1.0
EPSILON = 1e-06

MESH = pl.DeviceIdType.MESH
ROWS = 16
UNROLL_LIMIT = 16


def repeat(first, last, body):
    if last - first <= UNROLL_LIMIT:
        for index in range(first, last):
            body(index)
    else:

        def step(index, carry):
            body(index)
            return carry

        lax.fori_loop(first, last, step, 0)


def kernel(
    n_dom,
    n_sub,
    seg_ref,
    drag_ref,
    stress_ref,
    send_ref,
    partner_ref,
    pos_ref,
    vel_ref,
    stage,
    held,
    numer,
    left_side,
    at_i,
    vel_i,
    acc,
    sources,
    applied_ref,
    drag8_ref,
    vel_tx,
    vel_rx,
    top1_tx,
    top1_rx,
    top2_tx,
    top2_rx,
    state_send,
    state_recv,
    vel_send,
    vel_recv,
    top1_send,
    top1_recv,
    top2_send,
    top2_recv,
):
    nb, _, width = seg_ref.shape
    slots = n_sub + n_dom - 1
    dom = lax.axis_index("dom")
    sub = lax.axis_index("sub")
    used = 3 * nb
    tail = nb * ROWS

    if n_dom <= UNROLL_LIMIT:
        dom_ids = [lax.rem(dom + k, n_dom) for k in range(n_dom)]
    sub_ids = [lax.rem(sub + k, n_sub) for k in range(n_sub)]

    def dom_id(k):
        return dom_ids[k] if isinstance(k, int) else lax.rem(dom + k, n_dom)

    def sub_id(k):
        return sub_ids[k] if isinstance(k, int) else lax.rem(sub + k, n_sub)

    barrier = pltpu.get_barrier_semaphore()

    def greet(dom_to, sub_to):
        pl.semaphore_signal(barrier, inc=1, device_id=(dom_to, sub_to), device_id_type=MESH)

    repeat(1, n_dom, lambda k: greet(dom_id(k), sub))
    repeat(1, n_sub, lambda k: greet(dom, sub_id(k)))

    held[0] = jnp.zeros((tail + 8, width), jnp.float32)
    for r in range(nb):
        for a in range(3):
            held[0, ROWS * r + 3 * a : ROWS * r + 3 * a + 3, :] = seg_ref[r, 6 + a : 7 + a, :] * seg_ref[r, 3:6, :]
        held[0, tail + 3 * r : tail + 3 * r + 3, :] = seg_ref[r, 0:3, :]
    products = [held[0, ROWS * r : ROWS * (r + 1), :] for r in range(nb)]
    position = held[0, tail : tail + 8, :]
    row_id = lax.broadcasted_iota(jnp.int32, (8, width), 0)
    lane = lax.broadcasted_iota(jnp.int32, (8, width), 1)

    def fill(q):
        sent = send_ref[0, q].astype(jnp.float32)
        partner = partner_ref[0, q].astype(jnp.float32)
        for r in range(nb):
            stage[q, ROWS * r : ROWS * (r + 1), :] = products[r]
        entries = jnp.where(row_id == used, sent, jnp.where(row_id == used + 1, partner, position))
        stage[q, tail : tail + 8, :] = entries

    repeat(0, n_dom, fill)

    def sub_copy(k):
        return pltpu.make_async_remote_copy(
            src_ref=held.at[0],
            dst_ref=held.at[k],
            send_sem=state_send.at[k],
            recv_sem=state_recv.at[k],
            device_id=(dom, sub_id(k)),
            device_id_type=MESH,
        )

    def dom_copy(k):
        slot = n_sub - 1 + k
        return pltpu.make_async_remote_copy(
            src_ref=stage.at[dom_id(k)],
            dst_ref=held.at[slot],
            send_sem=state_send.at[slot],
            recv_sem=state_recv.at[slot],
            device_id=(dom_id(k), sub),
            device_id_type=MESH,
        )

    pl.semaphore_wait(barrier, slots - 1)
    repeat(1, n_dom, lambda k: dom_copy(k).start())
    repeat(1, n_sub, lambda k: sub_copy(k).start())

    applied_ref[...] = jnp.zeros((8, width), jnp.float32)
    drag8_ref[...] = jnp.ones((8, width), jnp.float32)
    for o in range(nb):
        b = [seg_ref[o, 6 + c : 7 + c, :] for c in range(3)]
        ln = [seg_ref[o, 3 + c : 4 + c, :] for c in range(3)]
        pulled = [
            stress_ref[c, 0] * b[0] + stress_ref[c, 1] * b[1] + stress_ref[c, 2] * b[2] for c in range(3)
        ]
        applied_ref[3 * o : 3 * o + 1, :] = pulled[1] * ln[2] - pulled[2] * ln[1]
        applied_ref[3 * o + 1 : 3 * o + 2, :] = pulled[2] * ln[0] - pulled[0] * ln[2]
        applied_ref[3 * o + 2 : 3 * o + 3, :] = pulled[0] * ln[1] - pulled[1] * ln[0]
        for c in range(3):
            drag8_ref[3 * o + c : 3 * o + c + 1, :] = drag_ref[o : o + 1, :]

    def split(value):
        high = value.astype(jnp.bfloat16)
        low = (value - high.astype(jnp.float32)).astype(jnp.bfloat16)
        return high, low

    def spread(target, tile):
        turned = tile.T
        for row in range(used):
            target[row] = jnp.broadcast_to(turned[:, row : row + 1], (width, width))

    spread(at_i, position)
    for o in range(nb):
        high = products[o].astype(jnp.bfloat16).astype(jnp.float32)
        low = products[o] - high
        left_side[o] = jnp.concatenate([high, high, low], axis=0).T.astype(jnp.bfloat16)

    def counts(base, peer, entries):
        table = []
        for o in range(nb):
            row = []
            for r in range(nb):
                value = jnp.full((1, width), base, jnp.float32)
                if peer is not None:
                    mine = jnp.logical_and(send_ref[0, peer] == o, partner_ref[0, peer] == r)
                    got, for_mine = entries
                    theirs = jnp.logical_and(got == float(r), for_mine == float(o))
                    value = value + jnp.where(mine, 1.0, 0.0) + jnp.where(theirs, 1.0, 0.0)
                row.append(value)
            table.append(row)
        return table

    def fill_numer(slot, base, peer, source=None, place=None):
        entries = None
        if peer is not None:
            entries = [source[place, tail + used + e : tail + used + e + 1, :] for e in range(2)]
        table = counts(base, peer, entries)
        for o in range(nb):
            pieces = [held[slot, ROWS * r : ROWS * (r + 1), :] * table[o][r] for r in range(nb)]
            high, low = split(jnp.concatenate(pieces, axis=1))
            numer[slot, o] = jnp.dot(
                left_side[o],
                jnp.concatenate([high, low, high], axis=0),
                preferred_element_type=jnp.float32,
            )

    def spread_sources(slot, tile):
        for row in range(used):
            sources[slot, row] = jnp.broadcast_to(tile[row : row + 1], (8, width))

    def add_slots(members, first, unroll, step=None):
        def chunk(g, carry):
            part = pl.ds(pl.multiple_of(8 * g, 8), 8)
            mine = [at_i[row, part, :] for row in range(used)]
            if step is not None:
                mine = [mine[row] + step * vel_i[row, part, :] for row in range(used)]
            total = [None if first else acc[row, part, :] for row in range(used)]

            def add_one(slot, total):
                total = list(total)
                for r in range(nb):
                    theirs = [sources[slot, 3 * r + c] for c in range(3)]
                    for o in range(nb):
                        off = [mine[3 * o + c] - theirs[c] for c in range(3)]
                        square = CORE_SQUARE + off[0] * off[0] + off[1] * off[1] + off[2] * off[2]
                        inverse = lax.rsqrt(square)
                        weight = numer[slot, o, part, pl.ds(width * r, width)] * inverse * (inverse * inverse)
                        for c in range(3):
                            term = weight * off[c]
                            row = 3 * o + c
                            total[row] = term if total[row] is None else total[row] + term
                return total

            if members[1] - members[0] <= UNROLL_LIMIT:
                for slot in range(*members):
                    total = add_one(slot, total)
            else:
                if first:
                    total = [jnp.zeros((8, width), jnp.float32)] * used
                total = lax.fori_loop(members[0], members[1], add_one, total)
            for row in range(used):
                acc[row, part, :] = total[row]
            return carry

        lax.fori_loop(0, width // 8, chunk, 0, unroll=unroll)

    def velocity_of(position):
        sums = [jnp.sum(acc[row].T, axis=0, keepdims=True) for row in range(used)]
        pair = jnp.concatenate(sums + [jnp.zeros((8 - used, width), jnp.float32)], axis=0)
        before = jnp.where(lane == 0, position, pltpu.roll(position, 1, 1))
        after = jnp.where(lane == width - 1, position, pltpu.roll(position, width - 1, 1))
        chain = before + after - 2.0 * position
        force = COUPLE * pair + applied_ref[...] + TENSION * chain
        velocity = force / drag8_ref[...]
        square = velocity * velocity
        tops = []
        for o in range(nb):
            tops.append(square[3 * o : 3 * o + 1] + square[3 * o + 1 : 3 * o + 2] + square[3 * o + 2 : 3 * o + 3])
        return velocity, functools.reduce(jnp.maximum, tops)

    def step_length(row):
        top = jnp.max(row, axis=1, keepdims=True)
        return STEP_LENGTH / (jnp.sqrt(top) + EPSILON)

    fill_numer(0, 1.0, dom, stage, dom)
    spread_sources(0, position)
    add_slots((0, 1), True, 2)

    def from_sub(k, carry):
        sub_copy(k).wait_recv()
        fill_numer(k, 1.0, None)
        spread_sources(k, held[k, tail : tail + 8, :])
        return carry

    def from_dom(k, carry):
        slot = n_sub - 1 + k
        dom_copy(k).wait_recv()
        fill_numer(slot, 0.0, lax.rem(dom - k + n_dom, n_dom), held, slot)
        spread_sources(slot, held[slot, tail : tail + 8, :])
        return carry

    lax.fori_loop(1, n_sub, from_sub, 0)
    add_slots((1, n_sub), False, 1)
    lax.fori_loop(1, n_dom, from_dom, 0)
    add_slots((n_sub, slots), False, 1)
    velocity, top = velocity_of(position)
    vel_tx[...] = jnp.where(row_id == used, top, velocity)
    top1_tx[...] = top

    def vel_copy(slot, dom_to, sub_to):
        return pltpu.make_async_remote_copy(
            src_ref=vel_tx,
            dst_ref=vel_rx.at[slot],
            send_sem=vel_send,
            recv_sem=vel_recv,
            device_id=(dom_to, sub_to),
            device_id_type=MESH,
        )

    def top1_copy(index):
        kd, ks = lax.div(index, n_sub - 1) + 1, lax.rem(index, n_sub - 1) + 1
        return pltpu.make_async_remote_copy(
            src_ref=top1_tx,
            dst_ref=top1_rx.at[index],
            send_sem=top1_send,
            recv_sem=top1_recv,
            device_id=(dom_id(kd), sub_id(ks)),
            device_id_type=MESH,
        )

    others = (n_sub - 1) * (n_dom - 1)
    repeat(1, n_dom, lambda k: vel_copy(n_sub - 1 + k, dom_id(k), sub).start())
    repeat(0, others, lambda k: top1_copy(k).start())
    repeat(1, n_sub, lambda k: vel_copy(k, dom, sub_id(k)).start())

    vel_rx[0] = vel_tx[...]
    spread(vel_i, velocity)

    arrived = vel_rx.at[pl.ds(1, slots - 1)]
    pltpu.make_async_copy(arrived, arrived, vel_recv).wait()
    pltpu.make_async_copy(top1_rx, top1_rx, top1_recv).wait()
    near = jnp.max(vel_rx[...], axis=0)[used : used + 1]
    far = jnp.max(top1_rx[...], axis=0)
    step = step_length(jnp.maximum(near, far))

    position = position + step * velocity

    def move(slot):
        spread_sources(slot, held[slot, tail : tail + 8, :] + step * vel_rx[slot])

    repeat(0, slots, move)
    add_slots((0, slots), True, 1, step)
    velocity, top = velocity_of(position)
    top2_tx[...] = top

    def top2_copy(index):
        kd, ks = lax.div(index + 1, n_sub), lax.rem(index + 1, n_sub)
        return pltpu.make_async_remote_copy(
            src_ref=top2_tx,
            dst_ref=top2_rx.at[index],
            send_sem=top2_send,
            recv_sem=top2_recv,
            device_id=(dom_id(kd), sub_id(ks)),
            device_id_type=MESH,
        )

    repeat(0, n_sub * n_dom - 1, lambda k: top2_copy(k).start())
    for o in range(nb):
        vel_ref[o] = velocity[3 * o : 3 * o + 3]

    repeat(1, n_sub, lambda k: sub_copy(k).wait_send())
    repeat(1, n_dom, lambda k: dom_copy(k).wait_send())
    pltpu.make_async_copy(arrived, arrived, vel_send).wait()
    pltpu.make_async_copy(top1_rx, top1_rx, top1_send).wait()

    pltpu.make_async_copy(top2_rx, top2_rx, top2_recv).wait()
    step = step_length(jnp.maximum(jnp.max(top2_rx[...], axis=0), top))
    position = position + step * velocity
    for o in range(nb):
        pos_ref[o] = position[3 * o : 3 * o + 3]
    pltpu.make_async_copy(top2_rx, top2_rx, top2_send).wait()


def solution(mesh):
    n_dom, n_sub = mesh.shape["dom"], mesh.shape["sub"]

    def local(segments, stress, drag_coef, send_ids, partner_ids):
        nb, _, width = segments.shape
        slots = n_sub + n_dom - 1
        rows = nb * ROWS + 8
        f32 = jnp.float32
        vmem = pl.BlockSpec(memory_space=pltpu.VMEM)
        out = jax.ShapeDtypeStruct((nb, 3, width), f32)
        words = slots * nb * width * nb * width + (n_dom + slots) * rows * width + 10 * nb * width * width
        words += 64 * slots * width
        dma = pltpu.SemaphoreType.DMA
        smem = pl.BlockSpec(memory_space=pltpu.SMEM)
        return pl.pallas_call(
            functools.partial(kernel, n_dom, n_sub),
            out_shape=(out, out),
            in_specs=[vmem, vmem, smem, smem, smem],
            out_specs=(vmem, vmem),
            scratch_shapes=[
                pltpu.VMEM((n_dom, rows, width), f32),
                pltpu.VMEM((slots, rows, width), f32),
                pltpu.VMEM((slots, nb, width, nb * width), f32),
                pltpu.VMEM((nb, width, 3 * ROWS), jnp.bfloat16),
                pltpu.VMEM((3 * nb, width, width), f32),
                pltpu.VMEM((3 * nb, width, width), f32),
                pltpu.VMEM((3 * nb, width, width), f32),
                pltpu.VMEM((slots, 3 * nb, 8, width), f32),
                pltpu.VMEM((8, width), f32),
                pltpu.VMEM((8, width), f32),
                pltpu.VMEM((8, width), f32),
                pltpu.VMEM((slots, 8, width), f32),
                pltpu.VMEM((1, width), f32),
                pltpu.VMEM(((n_dom - 1) * (n_sub - 1), 1, width), f32),
                pltpu.VMEM((1, width), f32),
                pltpu.VMEM((n_dom * n_sub - 1, 1, width), f32),
                dma((slots,)),
                dma((slots,)),
                dma,
                dma,
                dma,
                dma,
                dma,
                dma,
            ],
            compiler_params=pltpu.CompilerParams(
                collective_id=0,
                has_side_effects=True,
                vmem_limit_bytes=4 * words + 8 * 1024 * 1024,
            ),
        )(
            segments,
            drag_coef,
            stress,
            send_ids.reshape(1, n_dom),
            partner_ids.reshape(1, n_dom),
        )

    in_specs = (
        P(("dom", "sub"), None, None),
        P(),
        P(("dom", "sub"), None),
        P(("dom", "sub"), None, None),
        P(("dom", "sub"), None, None),
    )
    out_specs = (P(("dom", "sub"), None, None), P(("dom", "sub"), None, None))
    return jax.shard_map(local, mesh=mesh, in_specs=in_specs, out_specs=out_specs, check_vma=False)
```

```python
import functools

import jax
import jax.numpy as jnp
from jax import lax
from jax.experimental import pallas as pl
from jax.experimental.pallas import tpu as pltpu
from jax.sharding import PartitionSpec as P

STEPS = 2
COUPLE = 0.0625
CORE_SQUARE = 0.5
TENSION = 0.25
STEP_LENGTH = 1.0
EPSILON = 1e-06

MESH = pl.DeviceIdType.MESH
ROWS = 16
XROW, SROW, PROW = 9, 12, 13
UNROLL_LIMIT = 64


def repeat(first, last, body):
    if last - first <= UNROLL_LIMIT:
        for index in range(first, last):
            body(index)
    else:

        def step(index, carry):
            body(index)
            return carry

        lax.fori_loop(first, last, step, 0)


def kernel(
    n_dom,
    n_sub,
    seg_ref,
    drag_ref,
    stress_ref,
    send_ref,
    partner_ref,
    pos_ref,
    vel_ref,
    stage,
    held,
    numer,
    left_side,
    at_i,
    vel_i,
    acc,
    vel_tx,
    vel_rx,
    top1_tx,
    top1_rx,
    top2_tx,
    top2_rx,
    top3_tx,
    top3_rx,
    state_send,
    state_recv,
    sub_send,
    sub_recv,
    vel_send,
    vel_recv,
    top1_send,
    top1_recv,
    top2_send,
    top2_recv,
    top3_send,
    top3_recv,
):
    nb, _, width = seg_ref.shape
    slots = n_sub + n_dom - 1
    dom = lax.axis_index("dom")
    sub = lax.axis_index("sub")

    def sub_at(k):
        return (dom, lax.rem(sub + k, n_sub))

    def dom_at(k):
        return (lax.rem(dom + k, n_dom), sub)

    barrier = pltpu.get_barrier_semaphore()

    def greet_sub(k):
        pl.semaphore_signal(barrier, inc=1, device_id=sub_at(k), device_id_type=MESH)

    def greet_dom(k):
        pl.semaphore_signal(barrier, inc=1, device_id=dom_at(k), device_id_type=MESH)

    repeat(1, n_sub, greet_sub)
    repeat(1, n_dom, greet_dom)

    products = []
    for r in range(nb):
        burgers = seg_ref[r, 6:9, :]
        rows = [burgers[a : a + 1] * seg_ref[r, 3:6, :] for a in range(3)]
        block = jnp.concatenate(rows + [jnp.zeros((ROWS - 9, width), jnp.float32)], axis=0)
        products.append(block)
        held[0, r] = block
        held[0, r, XROW : XROW + 3, :] = seg_ref[r, 0:3, :]

    whole = [held[0, r] for r in range(nb)]
    row_id = lax.broadcasted_iota(jnp.int32, (ROWS, width), 0)

    def fill(q):
        sent = send_ref[0, q].astype(jnp.float32)
        partner = partner_ref[0, q].astype(jnp.float32)
        for r in range(nb):
            stage[q, r] = jnp.where(row_id == SROW, sent, jnp.where(row_id == PROW, partner, whole[r]))

    repeat(0, n_dom, fill)

    def sub_copy(k):
        return pltpu.make_async_remote_copy(
            src_ref=held.at[0],
            dst_ref=held.at[k],
            send_sem=state_send.at[k],
            recv_sem=state_recv.at[k],
            device_id=sub_at(k),
            device_id_type=MESH,
        )

    def dom_copy(k):
        slot = n_sub - 1 + k
        return pltpu.make_async_remote_copy(
            src_ref=stage.at[lax.rem(dom + k, n_dom)],
            dst_ref=held.at[slot],
            send_sem=state_send.at[slot],
            recv_sem=state_recv.at[slot],
            device_id=dom_at(k),
            device_id_type=MESH,
        )

    pl.semaphore_wait(barrier, slots - 1)
    repeat(1, n_dom, lambda k: dom_copy(k).start())
    repeat(1, n_sub, lambda k: sub_copy(k).start())

    applied_rows = []
    drag_rows = []
    for o in range(nb):
        b = [seg_ref[o, 6 + c : 7 + c, :] for c in range(3)]
        ln = [seg_ref[o, 3 + c : 4 + c, :] for c in range(3)]
        pulled = [
            stress_ref[c, 0] * b[0] + stress_ref[c, 1] * b[1] + stress_ref[c, 2] * b[2] for c in range(3)
        ]
        applied_rows.append(pulled[1] * ln[2] - pulled[2] * ln[1])
        applied_rows.append(pulled[2] * ln[0] - pulled[0] * ln[2])
        applied_rows.append(pulled[0] * ln[1] - pulled[1] * ln[0])
        drag_rows.extend([drag_ref[o : o + 1, :]] * 3)
    spare = 8 - 3 * nb
    zeros = jnp.zeros((spare, width), jnp.float32)
    applied = jnp.concatenate(applied_rows + [zeros], axis=0)
    drag = jnp.concatenate(drag_rows + [zeros + 1.0], axis=0)
    position = jnp.concatenate([seg_ref[o, 0:3, :] for o in range(nb)] + [zeros], axis=0)
    lane = lax.broadcasted_iota(jnp.int32, (8, width), 1)

    def split(value):
        high = value.astype(jnp.bfloat16)
        low = (value - high.astype(jnp.float32)).astype(jnp.bfloat16)
        return high, low

    for o in range(nb):
        high = products[o].astype(jnp.bfloat16).astype(jnp.float32)
        low = products[o] - high
        left_side[o] = jnp.concatenate([high, high, low], axis=0).T.astype(jnp.bfloat16)
        turned = whole[o].T
        for c in range(3):
            at_i[o, c] = jnp.broadcast_to(turned[:, XROW + c : XROW + c + 1], (width, width))

    def counts(slot, base, peer):
        table = []
        for o in range(nb):
            row = []
            for r in range(nb):
                value = jnp.full((1, width), base, jnp.float32)
                if peer is not None:
                    sent, partner = send_ref[0, peer], partner_ref[0, peer]
                    mine = jnp.logical_and(sent == o, partner == r)
                    value = value + jnp.where(mine, 1.0, 0.0)
                    source = stage if slot is None else held
                    place = dom if slot is None else slot
                    got, for_mine = source[place, 0, SROW : SROW + 1, :], source[place, 0, PROW : PROW + 1, :]
                    value = value + jnp.where(
                        jnp.logical_and(got == float(r), for_mine == float(o)), 1.0, 0.0
                    )
                row.append(value)
            table.append(row)
        return table

    def fill_numer(slot, base, peer):
        where = 0 if slot is None else slot
        table = counts(slot, base, peer)
        for o in range(nb):
            right = jnp.concatenate([held[where, r] * table[o][r] for r in range(nb)], axis=1)
            high, low = split(right)
            numer[where, o] = jnp.dot(
                left_side[o],
                jnp.concatenate([high, low, high], axis=0),
                preferred_element_type=jnp.float32,
            )

    def add_slot(slot, step, first=False):
        rows = []
        for r in range(nb):
            for c in range(3):
                row = held[slot, r, XROW + c : XROW + c + 1, :]
                if step is not None:
                    row = row + step * vel_rx[slot, r * 3 + c : r * 3 + c + 1, :]
                rows.append(jnp.broadcast_to(row, (8, width)))
        for o in range(nb):
            for g in range(width // 8):
                part = pl.ds(8 * g, 8)
                mine = [at_i[o, c, part, :] for c in range(3)]
                total = None if first else [acc[o, c, part, :] for c in range(3)]
                for r in range(nb):
                    off = [mine[c] - rows[r * 3 + c] for c in range(3)]
                    square = CORE_SQUARE + off[0] * off[0] + off[1] * off[1] + off[2] * off[2]
                    inverse = lax.rsqrt(square)
                    weight = numer[slot, o, part, pl.ds(width * r, width)] * inverse * (inverse * inverse)
                    terms = [weight * off[c] for c in range(3)]
                    total = terms if total is None else [total[c] + terms[c] for c in range(3)]
                for c in range(3):
                    acc[o, c, part, :] = total[c]

    def velocity_of(position):
        sums = []
        for o in range(nb):
            for c in range(3):
                sums.append(jnp.sum(acc[o, c].T, axis=0, keepdims=True))
        pair = jnp.concatenate(sums + [zeros], axis=0)
        before = jnp.where(lane == 0, position, pltpu.roll(position, 1, 1))
        after = jnp.where(lane == width - 1, position, pltpu.roll(position, width - 1, 1))
        chain = before + after - 2.0 * position
        force = COUPLE * pair + applied + TENSION * chain
        velocity = force / drag
        square = velocity * velocity
        tops = []
        for o in range(nb):
            tops.append(square[3 * o : 3 * o + 1] + square[3 * o + 1 : 3 * o + 2] + square[3 * o + 2 : 3 * o + 3])
        return velocity, functools.reduce(jnp.maximum, tops)

    def step_length(row):
        top = jnp.max(row, axis=1, keepdims=True)
        return STEP_LENGTH / (jnp.sqrt(top) + EPSILON)

    fill_numer(None, 1.0, dom)
    add_slot(0, None, first=True)

    def from_sub(k, carry):
        sub_copy(k).wait_recv()
        fill_numer(k, 1.0, None)
        add_slot(k, None)
        return carry

    def from_dom(k, carry):
        slot = n_sub - 1 + k
        dom_copy(k).wait_recv()
        fill_numer(slot, 0.0, lax.rem(dom - k + n_dom, n_dom))
        add_slot(slot, None)
        return carry

    lax.fori_loop(1, n_sub, from_sub, 0)
    lax.fori_loop(1, n_dom, from_dom, 0)
    velocity, top = velocity_of(position)
    vel_tx[...] = jnp.concatenate([velocity[0 : 3 * nb], top, zeros[: spare - 1]], axis=0)

    def send(source, target, send_sem, recv_sem, device):
        return pltpu.make_async_remote_copy(
            src_ref=source,
            dst_ref=target,
            send_sem=send_sem,
            recv_sem=recv_sem,
            device_id=device,
            device_id_type=MESH,
        )

    def all_of(buffer, sem):
        return pltpu.make_async_copy(buffer, buffer, sem)

    def to_row(source, buffer, first, send_sem, recv_sem):
        repeat(1, n_sub, lambda k: send(source, buffer.at[first + k], send_sem, recv_sem, sub_at(k)).start())

    def to_column(source, buffer, first, send_sem, recv_sem):
        repeat(1, n_dom, lambda k: send(source, buffer.at[first + k], send_sem, recv_sem, dom_at(k)).start())

    from_row = vel_rx.at[pl.ds(1, n_sub - 1)]
    from_column = vel_rx.at[pl.ds(n_sub, n_dom - 1)]
    to_row(vel_tx, vel_rx, 0, sub_send, sub_recv)
    to_column(vel_tx, vel_rx, n_sub - 1, vel_send, vel_recv)

    vel_rx[0] = vel_tx[...]
    all_of(from_row, sub_recv).wait()
    row_top = jnp.max(vel_rx[0:n_sub], axis=0)[3 * nb : 3 * nb + 1]
    top1_tx[...] = row_top
    to_column(top1_tx, top1_rx, -1, top1_send, top1_recv)

    turned = velocity.T
    for o in range(nb):
        for c in range(3):
            vel_i[o, c] = jnp.broadcast_to(turned[:, 3 * o + c : 3 * o + c + 1], (width, width))

    all_of(from_column, vel_recv).wait()
    all_of(top1_rx, top1_recv).wait()
    step = step_length(jnp.maximum(row_top, jnp.max(top1_rx[...], axis=0)))

    position = position + step * velocity
    for o in range(nb):
        for c in range(3):
            at_i[o, c] = at_i[o, c] + step * vel_i[o, c]
    add_slot(0, step, first=True)

    def again(slot, carry):
        add_slot(slot, carry)
        return carry

    lax.fori_loop(1, slots, again, step)
    velocity, top = velocity_of(position)
    top2_tx[...] = top

    to_row(top2_tx, top2_rx, -1, top2_send, top2_recv)
    for o in range(nb):
        vel_ref[o] = velocity[3 * o : 3 * o + 3]

    all_of(top2_rx, top2_recv).wait()
    row_top = jnp.maximum(jnp.max(top2_rx[...], axis=0), top)
    top3_tx[...] = row_top
    to_column(top3_tx, top3_rx, -1, top3_send, top3_recv)

    repeat(1, n_sub, lambda k: sub_copy(k).wait_send())
    repeat(1, n_dom, lambda k: dom_copy(k).wait_send())
    all_of(from_row, sub_send).wait()
    all_of(from_column, vel_send).wait()
    all_of(top1_rx, top1_send).wait()
    all_of(top2_rx, top2_send).wait()

    all_of(top3_rx, top3_recv).wait()
    step = step_length(jnp.maximum(row_top, jnp.max(top3_rx[...], axis=0)))
    position = position + step * velocity
    for o in range(nb):
        pos_ref[o] = position[3 * o : 3 * o + 3]
    all_of(top3_rx, top3_send).wait()


def solution(mesh):
    n_dom, n_sub = mesh.shape["dom"], mesh.shape["sub"]

    def local(segments, stress, drag_coef, send_ids, partner_ids):
        nb, _, width = segments.shape
        slots = n_sub + n_dom - 1
        f32 = jnp.float32
        vmem = pl.BlockSpec(memory_space=pltpu.VMEM)
        smem = pl.BlockSpec(memory_space=pltpu.SMEM)
        out = jax.ShapeDtypeStruct((nb, 3, width), f32)
        words = slots * nb * width * nb * width + (n_dom + slots) * nb * ROWS * width + 9 * nb * width * width
        return pl.pallas_call(
            functools.partial(kernel, n_dom, n_sub),
            out_shape=(out, out),
            in_specs=[vmem, vmem, smem, smem, smem],
            out_specs=(vmem, vmem),
            scratch_shapes=[
                pltpu.VMEM((n_dom, nb, ROWS, width), f32),
                pltpu.VMEM((slots, nb, ROWS, width), f32),
                pltpu.VMEM((slots, nb, width, nb * width), f32),
                pltpu.VMEM((nb, width, 3 * ROWS), jnp.bfloat16),
                pltpu.VMEM((nb, 3, width, width), f32),
                pltpu.VMEM((nb, 3, width, width), f32),
                pltpu.VMEM((nb, 3, width, width), f32),
                pltpu.VMEM((8, width), f32),
                pltpu.VMEM((slots, 8, width), f32),
                pltpu.VMEM((1, width), f32),
                pltpu.VMEM((n_dom - 1, 1, width), f32),
                pltpu.VMEM((1, width), f32),
                pltpu.VMEM((n_sub - 1, 1, width), f32),
                pltpu.VMEM((1, width), f32),
                pltpu.VMEM((n_dom - 1, 1, width), f32),
                pltpu.SemaphoreType.DMA((slots,)),
                pltpu.SemaphoreType.DMA((slots,)),
                pltpu.SemaphoreType.DMA,
                pltpu.SemaphoreType.DMA,
                pltpu.SemaphoreType.DMA,
                pltpu.SemaphoreType.DMA,
                pltpu.SemaphoreType.DMA,
                pltpu.SemaphoreType.DMA,
                pltpu.SemaphoreType.DMA,
                pltpu.SemaphoreType.DMA,
                pltpu.SemaphoreType.DMA,
                pltpu.SemaphoreType.DMA,
            ],
            compiler_params=pltpu.CompilerParams(
                collective_id=0,
                has_side_effects=True,
                vmem_limit_bytes=4 * words + 8 * 1024 * 1024,
            ),
        )(
            segments,
            drag_coef,
            stress,
            send_ids.reshape(1, n_dom),
            partner_ids.reshape(1, n_dom),
        )

    in_specs = (
        P(("dom", "sub"), None, None),
        P(),
        P(("dom", "sub"), None),
        P(("dom", "sub"), None, None),
        P(("dom", "sub"), None, None),
    )
    out_specs = (P(("dom", "sub"), None, None), P(("dom", "sub"), None, None))
    return jax.shard_map(local, mesh=mesh, in_specs=in_specs, out_specs=out_specs, check_vma=False)
```

```python
import functools

import jax
import jax.numpy as jnp
from jax import lax
from jax.experimental import pallas as pl
from jax.experimental.pallas import tpu as pltpu
from jax.sharding import PartitionSpec as P

STEPS = 2
COUPLE = 0.0625
CORE_SQUARE = 0.5
TENSION = 0.25
STEP_LENGTH = 1.0
EPSILON = 1e-06

MESH = pl.DeviceIdType.MESH
DEPTH = 80
UNROLL_LIMIT = 64


def repeat(first, last, body):
    if last - first <= UNROLL_LIMIT:
        for index in range(first, last):
            body(index)
    else:

        def step(index, carry):
            body(index)
            return carry

        lax.fori_loop(first, last, step, 0)


def kernel(
    n_dom,
    n_sub,
    seg_ref,
    drag_ref,
    stress_ref,
    send_ref,
    partner_ref,
    pos_ref,
    vel_ref,
    stage,
    held,
    numer,
    left_side,
    at_i,
    vel_i,
    acc,
    vel_tx,
    vel_rx,
    top1_tx,
    top1_rx,
    top2_tx,
    top2_rx,
    state_send,
    state_recv,
    vel_send,
    vel_recv,
    top1_send,
    top1_recv,
    top2_send,
    top2_recv,
):
    nb, _, width = seg_ref.shape
    slots = n_sub + n_dom - 1
    dom = lax.axis_index("dom")
    sub = lax.axis_index("sub")

    def sub_at(k):
        return (dom, lax.rem(sub + k, n_sub))

    def dom_at(k):
        return (lax.rem(dom + k, n_dom), sub)

    barrier = pltpu.get_barrier_semaphore()

    def greet_sub(k):
        pl.semaphore_signal(barrier, inc=1, device_id=sub_at(k), device_id_type=MESH)

    def greet_dom(k):
        pl.semaphore_signal(barrier, inc=1, device_id=dom_at(k), device_id_type=MESH)

    repeat(1, n_sub, greet_sub)
    repeat(1, n_dom, greet_dom)

    used = 3 * nb
    srow, prow, brow, lrow = used, used + 1, used + 2, 2 * used + 2
    for r in range(nb):
        for first, source in ((0, 0), (brow, 6), (lrow, 3)):
            held[0, first + 3 * r : first + 3 * r + 3, :] = seg_ref[r, source : source + 3, :]
    held[0, srow : prow + 1, :] = jnp.zeros((2, width), jnp.float32)
    whole = held[0]
    row_id = lax.broadcasted_iota(jnp.int32, whole.shape, 0)

    def fill(q):
        sent = send_ref[0, q].astype(jnp.float32)
        partner = partner_ref[0, q].astype(jnp.float32)
        stage[q] = jnp.where(row_id == srow, sent, jnp.where(row_id == prow, partner, whole))

    repeat(0, n_dom, fill)

    def sub_copy(k):
        return pltpu.make_async_remote_copy(
            src_ref=held.at[0],
            dst_ref=held.at[k],
            send_sem=state_send.at[k],
            recv_sem=state_recv.at[k],
            device_id=sub_at(k),
            device_id_type=MESH,
        )

    def dom_copy(k):
        slot = n_sub - 1 + k
        return pltpu.make_async_remote_copy(
            src_ref=stage.at[lax.rem(dom + k, n_dom)],
            dst_ref=held.at[slot],
            send_sem=state_send.at[slot],
            recv_sem=state_recv.at[slot],
            device_id=dom_at(k),
            device_id_type=MESH,
        )

    pl.semaphore_wait(barrier, slots - 1)
    repeat(1, n_dom, lambda k: dom_copy(k).start())
    repeat(1, n_sub, lambda k: sub_copy(k).start())

    applied_rows = []
    drag_rows = []
    for o in range(nb):
        b = [seg_ref[o, 6 + c : 7 + c, :] for c in range(3)]
        ln = [seg_ref[o, 3 + c : 4 + c, :] for c in range(3)]
        pulled = [
            stress_ref[c, 0] * b[0] + stress_ref[c, 1] * b[1] + stress_ref[c, 2] * b[2] for c in range(3)
        ]
        applied_rows.append(pulled[1] * ln[2] - pulled[2] * ln[1])
        applied_rows.append(pulled[2] * ln[0] - pulled[0] * ln[2])
        applied_rows.append(pulled[0] * ln[1] - pulled[1] * ln[0])
        drag_rows.extend([drag_ref[o : o + 1, :]] * 3)
    spare = 8 - 3 * nb
    zeros = jnp.zeros((spare, width), jnp.float32)
    applied = jnp.concatenate(applied_rows + [zeros], axis=0)
    drag = jnp.concatenate(drag_rows + [zeros + 1.0], axis=0)
    position = jnp.concatenate([seg_ref[o, 0:3, :] for o in range(nb)] + [zeros], axis=0)
    lane = lax.broadcasted_iota(jnp.int32, (8, width), 1)
    tile_row = lax.broadcasted_iota(jnp.int32, (8, width), 0)
    diagonal = lax.broadcasted_iota(jnp.int32, (width, width), 0) == lax.broadcasted_iota(
        jnp.int32, (width, width), 1
    )

    def split(value):
        high = value.astype(jnp.bfloat16)
        low = (value - high.astype(jnp.float32)).astype(jnp.bfloat16)
        return high, low

    for o in range(nb):
        lines = jnp.concatenate([seg_ref[o, 3:6, :]] * nb + [zeros], axis=0)
        product = jnp.concatenate([seg_ref[o, 6 + a : 7 + a, :] * lines for a in range(3)], axis=0)
        high = product.astype(jnp.bfloat16).astype(jnp.float32)
        rest = jnp.zeros((DEPTH - 72, width), jnp.float32)
        left_side[o] = jnp.concatenate([high, high, product - high, rest], axis=0).T.astype(jnp.bfloat16)
    turned = position.T
    for o in range(nb):
        for c in range(3):
            at_i[o, c] = jnp.broadcast_to(turned[:, 3 * o + c : 3 * o + c + 1], (width, width))

    def counts(slot, base, peer):
        table = []
        for o in range(nb):
            row = []
            for r in range(nb):
                value = jnp.full((1, width), base, jnp.float32)
                if peer is not None:
                    sent, partner = send_ref[0, peer], partner_ref[0, peer]
                    mine = jnp.logical_and(sent == o, partner == r)
                    value = value + jnp.where(mine, 1.0, 0.0)
                    source = stage if slot is None else held
                    place = dom if slot is None else slot
                    got, for_mine = source[place, srow : srow + 1, :], source[place, prow : prow + 1, :]
                    value = value + jnp.where(
                        jnp.logical_and(got == float(r), for_mine == float(o)), 1.0, 0.0
                    )
                row.append(value)
            table.append(row)
        return table

    def fill_numer(slot, base, peer):
        where = 0 if slot is None else slot
        table = counts(slot, base, peer)
        lines = jnp.concatenate([held[where, lrow : lrow + used, :], zeros], axis=0)
        pieces = []
        for r in range(nb):
            here = jnp.logical_and(tile_row >= 3 * r, tile_row < 3 * r + 3)
            own_lines = jnp.where(here, lines, 0.0)
            b = [held[where, brow + 3 * r + a : brow + 3 * r + a + 1, :] for a in range(3)]
            pieces.append(jnp.concatenate([b[a] * own_lines for a in range(3)], axis=0))
        for o in range(nb):
            right = jnp.concatenate([pieces[r] * table[o][r] for r in range(nb)], axis=1)
            high = right.astype(jnp.bfloat16).astype(jnp.float32)
            rest = jnp.zeros((DEPTH - 72, nb * width), jnp.float32)
            stack = jnp.concatenate([high, right - high, high, rest], axis=0)
            numer[where, o] = jnp.dot(
                left_side[o], stack.astype(jnp.bfloat16), preferred_element_type=jnp.float32
            )

    def add_slot(slot, step, first=False):
        rows = []
        for r in range(nb):
            for c in range(3):
                row = held[slot, 3 * r + c : 3 * r + c + 1, :]
                if step is not None:
                    row = row + step * vel_rx[slot, r * 3 + c : r * 3 + c + 1, :]
                rows.append(jnp.broadcast_to(row, (8, width)))
        for o in range(nb):
            for g in range(width // 8):
                part = pl.ds(8 * g, 8)
                mine = [at_i[o, c, part, :] for c in range(3)]
                total = None if first else [acc[o, c, part, :] for c in range(3)]
                for r in range(nb):
                    off = [mine[c] - rows[r * 3 + c] for c in range(3)]
                    square = CORE_SQUARE + off[0] * off[0] + off[1] * off[1] + off[2] * off[2]
                    inverse = lax.rsqrt(square)
                    weight = numer[slot, o, part, pl.ds(width * r, width)] * inverse * (inverse * inverse)
                    terms = [weight * off[c] for c in range(3)]
                    total = terms if total is None else [total[c] + terms[c] for c in range(3)]
                for c in range(3):
                    acc[o, c, part, :] = total[c]

    def velocity_of(position):
        high, low = split(acc[...].reshape(used * width, width))
        lane_sums = jnp.dot(
            jnp.concatenate([high, low], axis=1),
            jnp.ones((2 * width, width), jnp.bfloat16),
            preferred_element_type=jnp.float32,
        ).reshape(used, width, width)
        sums = [
            jnp.sum(jnp.where(diagonal, lane_sums[row], 0.0), axis=0, keepdims=True) for row in range(used)
        ]
        pair = jnp.concatenate(sums + [zeros], axis=0)
        before = jnp.where(lane == 0, position, pltpu.roll(position, 1, 1))
        after = jnp.where(lane == width - 1, position, pltpu.roll(position, width - 1, 1))
        chain = before + after - 2.0 * position
        force = COUPLE * pair + applied + TENSION * chain
        velocity = force / drag
        square = velocity * velocity
        tops = []
        for o in range(nb):
            tops.append(square[3 * o : 3 * o + 1] + square[3 * o + 1 : 3 * o + 2] + square[3 * o + 2 : 3 * o + 3])
        return velocity, functools.reduce(jnp.maximum, tops)

    def step_length(row):
        top = jnp.max(row, axis=1, keepdims=True)
        return STEP_LENGTH / (jnp.sqrt(top) + EPSILON)

    fill_numer(None, 1.0, dom)
    add_slot(0, None, first=True)

    def from_sub(k, carry):
        sub_copy(k).wait_recv()
        fill_numer(k, 1.0, None)
        add_slot(k, None)
        return carry

    def from_dom(k, carry):
        slot = n_sub - 1 + k
        dom_copy(k).wait_recv()
        fill_numer(slot, 0.0, lax.rem(dom - k + n_dom, n_dom))
        add_slot(slot, None)
        return carry

    lax.fori_loop(1, n_sub, from_sub, 0)
    lax.fori_loop(1, n_dom, from_dom, 0)
    velocity, top = velocity_of(position)
    vel_tx[...] = jnp.concatenate([velocity[0 : 3 * nb], top, zeros[: spare - 1]], axis=0)
    top1_tx[...] = top

    def vel_copy(slot, target):
        return pltpu.make_async_remote_copy(
            src_ref=vel_tx,
            dst_ref=vel_rx.at[slot],
            send_sem=vel_send,
            recv_sem=vel_recv,
            device_id=target,
            device_id_type=MESH,
        )

    def top1_copy(index):
        kd, ks = index // (n_sub - 1) + 1, index % (n_sub - 1) + 1
        return pltpu.make_async_remote_copy(
            src_ref=top1_tx,
            dst_ref=top1_rx.at[index],
            send_sem=top1_send,
            recv_sem=top1_recv,
            device_id=(lax.rem(dom + kd, n_dom), lax.rem(sub + ks, n_sub)),
            device_id_type=MESH,
        )

    others = (n_sub - 1) * (n_dom - 1)
    repeat(1, n_dom, lambda k: vel_copy(n_sub - 1 + k, dom_at(k)).start())
    repeat(0, others, lambda k: top1_copy(k).start())
    repeat(1, n_sub, lambda k: vel_copy(k, sub_at(k)).start())

    vel_rx[0] = vel_tx[...]
    turned = velocity.T
    for o in range(nb):
        for c in range(3):
            vel_i[o, c] = jnp.broadcast_to(turned[:, 3 * o + c : 3 * o + c + 1], (width, width))

    arrived = vel_rx.at[pl.ds(1, slots - 1)]
    pltpu.make_async_copy(arrived, arrived, vel_recv).wait()
    pltpu.make_async_copy(top1_rx, top1_rx, top1_recv).wait()
    near = jnp.max(vel_rx[:, 3 * nb : 3 * nb + 1, :], axis=0)
    far = jnp.max(top1_rx[...], axis=0)
    step = step_length(jnp.maximum(near, far))

    position = position + step * velocity
    for o in range(nb):
        for c in range(3):
            at_i[o, c] = at_i[o, c] + step * vel_i[o, c]
    add_slot(0, step, first=True)

    def again(slot, carry):
        add_slot(slot, carry)
        return carry

    lax.fori_loop(1, slots, again, step)
    velocity, top = velocity_of(position)
    top2_tx[...] = top

    def top2_copy(index):
        kd, ks = (index + 1) // n_sub, (index + 1) % n_sub
        return pltpu.make_async_remote_copy(
            src_ref=top2_tx,
            dst_ref=top2_rx.at[index],
            send_sem=top2_send,
            recv_sem=top2_recv,
            device_id=(lax.rem(dom + kd, n_dom), lax.rem(sub + ks, n_sub)),
            device_id_type=MESH,
        )

    repeat(0, n_sub * n_dom - 1, lambda k: top2_copy(k).start())
    for o in range(nb):
        vel_ref[o] = velocity[3 * o : 3 * o + 3]

    repeat(1, n_sub, lambda k: sub_copy(k).wait_send())
    repeat(1, n_dom, lambda k: dom_copy(k).wait_send())
    pltpu.make_async_copy(arrived, arrived, vel_send).wait()
    pltpu.make_async_copy(top1_rx, top1_rx, top1_send).wait()

    pltpu.make_async_copy(top2_rx, top2_rx, top2_recv).wait()
    step = step_length(jnp.maximum(jnp.max(top2_rx[...], axis=0), top))
    position = position + step * velocity
    for o in range(nb):
        pos_ref[o] = position[3 * o : 3 * o + 3]
    pltpu.make_async_copy(top2_rx, top2_rx, top2_send).wait()


def solution(mesh):
    n_dom, n_sub = mesh.shape["dom"], mesh.shape["sub"]

    def local(segments, stress, drag_coef, send_ids, partner_ids):
        nb, _, width = segments.shape
        slots = n_sub + n_dom - 1
        f32 = jnp.float32
        vmem = pl.BlockSpec(memory_space=pltpu.VMEM)
        smem = pl.BlockSpec(memory_space=pltpu.SMEM)
        out = jax.ShapeDtypeStruct((nb, 3, width), f32)
        rows = 9 * nb + 2
        words = slots * nb * width * nb * width + (n_dom + slots) * (rows + 8) * width + 9 * nb * width * width
        return pl.pallas_call(
            functools.partial(kernel, n_dom, n_sub),
            out_shape=(out, out),
            in_specs=[vmem, vmem, smem, smem, smem],
            out_specs=(vmem, vmem),
            scratch_shapes=[
                pltpu.VMEM((n_dom, rows, width), f32),
                pltpu.VMEM((slots, rows, width), f32),
                pltpu.VMEM((slots, nb, width, nb * width), f32),
                pltpu.VMEM((nb, width, DEPTH), jnp.bfloat16),
                pltpu.VMEM((nb, 3, width, width), f32),
                pltpu.VMEM((nb, 3, width, width), f32),
                pltpu.VMEM((nb, 3, width, width), f32),
                pltpu.VMEM((8, width), f32),
                pltpu.VMEM((slots, 8, width), f32),
                pltpu.VMEM((1, width), f32),
                pltpu.VMEM(((n_dom - 1) * (n_sub - 1), 1, width), f32),
                pltpu.VMEM((1, width), f32),
                pltpu.VMEM((n_dom * n_sub - 1, 1, width), f32),
                pltpu.SemaphoreType.DMA((slots,)),
                pltpu.SemaphoreType.DMA((slots,)),
                pltpu.SemaphoreType.DMA,
                pltpu.SemaphoreType.DMA,
                pltpu.SemaphoreType.DMA,
                pltpu.SemaphoreType.DMA,
                pltpu.SemaphoreType.DMA,
                pltpu.SemaphoreType.DMA,
            ],
            compiler_params=pltpu.CompilerParams(
                collective_id=0,
                has_side_effects=True,
                vmem_limit_bytes=4 * words + 8 * 1024 * 1024,
            ),
        )(
            segments,
            drag_coef,
            stress,
            send_ids.reshape(1, n_dom),
            partner_ids.reshape(1, n_dom),
        )

    in_specs = (
        P(("dom", "sub"), None, None),
        P(),
        P(("dom", "sub"), None),
        P(("dom", "sub"), None, None),
        P(("dom", "sub"), None, None),
    )
    out_specs = (P(("dom", "sub"), None, None), P(("dom", "sub"), None, None))
    return jax.shard_map(local, mesh=mesh, in_specs=in_specs, out_specs=out_specs, check_vma=False)
```

```python
import functools

import jax
import jax.numpy as jnp
from jax import lax
from jax.experimental import pallas as pl
from jax.experimental.pallas import tpu as pltpu
from jax.sharding import PartitionSpec as P

STEPS = 2
COUPLE = 0.0625
CORE_SQUARE = 0.5
TENSION = 0.25
STEP_LENGTH = 1.0
EPSILON = 1e-06

MESH = pl.DeviceIdType.MESH
DEPTH = 80
UNROLL_LIMIT = 64


def repeat(first, last, body):
    if last - first <= UNROLL_LIMIT:
        for index in range(first, last):
            body(index)
    else:

        def step(index, carry):
            body(index)
            return carry

        lax.fori_loop(first, last, step, 0)


def kernel(
    n_dom,
    n_sub,
    seg_ref,
    drag_ref,
    stress_ref,
    send_ref,
    partner_ref,
    pos_ref,
    vel_ref,
    stage,
    held,
    numer_even,
    numer_odd,
    left_side,
    at_i,
    vel_i,
    acc,
    vel_tx,
    vel_rx,
    top1_tx,
    top1_rx,
    top2_tx,
    top2_rx,
    state_send,
    state_recv,
    vel_send,
    vel_recv,
    top1_send,
    top1_recv,
    top2_send,
    top2_recv,
):
    nb, _, width = seg_ref.shape
    slots = n_sub + n_dom - 1
    dom = lax.axis_index("dom")
    sub = lax.axis_index("sub")

    def sub_at(k):
        return (dom, lax.rem(sub + k, n_sub))

    def dom_at(k):
        return (lax.rem(dom + k, n_dom), sub)

    barrier = pltpu.get_barrier_semaphore()

    def greet_sub(k):
        pl.semaphore_signal(barrier, inc=1, device_id=sub_at(k), device_id_type=MESH)

    def greet_dom(k):
        pl.semaphore_signal(barrier, inc=1, device_id=dom_at(k), device_id_type=MESH)

    repeat(1, n_sub, greet_sub)
    repeat(1, n_dom, greet_dom)

    used = 3 * nb
    srow, prow, brow, lrow = used, used + 1, used + 2, 2 * used + 2
    for r in range(nb):
        for first, source in ((0, 0), (brow, 6), (lrow, 3)):
            held[0, first + 3 * r : first + 3 * r + 3, :] = seg_ref[r, source : source + 3, :]
    held[0, srow : prow + 1, :] = jnp.full((2, width), -1.0, jnp.float32)
    whole = held[0]
    row_id = lax.broadcasted_iota(jnp.int32, whole.shape, 0)

    def fill(q):
        sent = send_ref[0, q].astype(jnp.float32)
        partner = partner_ref[0, q].astype(jnp.float32)
        stage[q] = jnp.where(row_id == srow, sent, jnp.where(row_id == prow, partner, whole))

    repeat(0, n_dom, fill)

    def sub_copy(k):
        return pltpu.make_async_remote_copy(
            src_ref=held.at[0],
            dst_ref=held.at[k],
            send_sem=state_send.at[k],
            recv_sem=state_recv.at[k],
            device_id=sub_at(k),
            device_id_type=MESH,
        )

    def dom_copy(k):
        slot = n_sub - 1 + k
        return pltpu.make_async_remote_copy(
            src_ref=stage.at[lax.rem(dom + k, n_dom)],
            dst_ref=held.at[slot],
            send_sem=state_send.at[slot],
            recv_sem=state_recv.at[slot],
            device_id=dom_at(k),
            device_id_type=MESH,
        )

    pl.semaphore_wait(barrier, slots - 1)
    repeat(1, n_dom, lambda k: dom_copy(k).start())
    repeat(1, n_sub, lambda k: sub_copy(k).start())

    applied_rows = []
    drag_rows = []
    for o in range(nb):
        b = [seg_ref[o, 6 + c : 7 + c, :] for c in range(3)]
        ln = [seg_ref[o, 3 + c : 4 + c, :] for c in range(3)]
        pulled = [
            stress_ref[c, 0] * b[0] + stress_ref[c, 1] * b[1] + stress_ref[c, 2] * b[2] for c in range(3)
        ]
        applied_rows.append(pulled[1] * ln[2] - pulled[2] * ln[1])
        applied_rows.append(pulled[2] * ln[0] - pulled[0] * ln[2])
        applied_rows.append(pulled[0] * ln[1] - pulled[1] * ln[0])
        drag_rows.extend([drag_ref[o : o + 1, :]] * 3)
    spare = 8 - 3 * nb
    zeros = jnp.zeros((spare, width), jnp.float32)
    applied = jnp.concatenate(applied_rows + [zeros], axis=0)
    drag = jnp.concatenate(drag_rows + [zeros + 1.0], axis=0)
    position = jnp.concatenate([seg_ref[o, 0:3, :] for o in range(nb)] + [zeros], axis=0)
    lane = lax.broadcasted_iota(jnp.int32, (8, width), 1)
    tile_row = lax.broadcasted_iota(jnp.int32, (8, width), 0)
    diagonal = lax.broadcasted_iota(jnp.int32, (width, width), 0) == lax.broadcasted_iota(
        jnp.int32, (width, width), 1
    )

    def split(value):
        high = value.astype(jnp.bfloat16)
        low = (value - high.astype(jnp.float32)).astype(jnp.bfloat16)
        return high, low

    for o in range(nb):
        lines = jnp.concatenate([seg_ref[o, 3:6, :]] * nb + [zeros], axis=0)
        product = jnp.concatenate([seg_ref[o, 6 + a : 7 + a, :] * lines for a in range(3)], axis=0)
        high = product.astype(jnp.bfloat16).astype(jnp.float32)
        rest = jnp.zeros((DEPTH - 72, width), jnp.float32)
        left_side[o] = jnp.concatenate([high, high, product - high, rest], axis=0).T.astype(jnp.bfloat16)
    turned = position.T
    for o in range(nb):
        for c in range(3):
            at_i[o, c] = jnp.broadcast_to(turned[:, 3 * o + c : 3 * o + c + 1], (width, width))

    def counts(base, sent, partner, got, for_mine):
        table = []
        for o in range(nb):
            row = []
            for r in range(nb):
                mine = jnp.logical_and(sent == o, partner == r)
                theirs = jnp.logical_and(got == float(r), for_mine == float(o))
                row.append(base + jnp.where(mine, 1.0, 0.0) + jnp.where(theirs, 1.0, 0.0))
            table.append(row)
        return table

    def fill_numer(where, numer):
        if isinstance(where, int):
            base, peer, listed = jnp.ones((1, width), jnp.float32), dom, True
            source, place = stage, dom
        else:
            base = jnp.full((1, width), jnp.where(where < n_sub, 1.0, 0.0), jnp.float32)
            listed = where >= n_sub
            peer = jnp.where(listed, lax.rem(dom - where + n_sub - 1 + n_dom, n_dom), 0)
            source, place = held, where
        sent = jnp.where(listed, send_ref[0, peer], -1)
        table = counts(
            base, sent, partner_ref[0, peer], source[place, srow : srow + 1, :], source[place, prow : prow + 1, :]
        )
        lines = jnp.concatenate([held[where, lrow : lrow + used, :], zeros], axis=0)
        pieces = []
        for r in range(nb):
            here = jnp.logical_and(tile_row >= 3 * r, tile_row < 3 * r + 3)
            own_lines = jnp.where(here, lines, 0.0)
            b = [held[where, brow + 3 * r + a : brow + 3 * r + a + 1, :] for a in range(3)]
            pieces.append(jnp.concatenate([b[a] * own_lines for a in range(3)], axis=0))
        for o in range(nb):
            right = jnp.concatenate([pieces[r] * table[o][r] for r in range(nb)], axis=1)
            high = right.astype(jnp.bfloat16).astype(jnp.float32)
            rest = jnp.zeros((DEPTH - 72, nb * width), jnp.float32)
            stack = jnp.concatenate([high, right - high, high, rest], axis=0)
            numer[o] = jnp.dot(
                left_side[o], stack.astype(jnp.bfloat16), preferred_element_type=jnp.float32
            )

    def add_slot(slot, numer, step, first=False):
        rows = []
        for r in range(nb):
            for c in range(3):
                row = held[slot, 3 * r + c : 3 * r + c + 1, :]
                if step is not None:
                    row = row + step * vel_rx[slot, r * 3 + c : r * 3 + c + 1, :]
                rows.append(jnp.broadcast_to(row, (8, width)))
        for o in range(nb):
            for g in range(width // 8):
                part = pl.ds(8 * g, 8)
                mine = [at_i[o, c, part, :] for c in range(3)]
                total = None if first else [acc[o, c, part, :] for c in range(3)]
                for r in range(nb):
                    off = [mine[c] - rows[r * 3 + c] for c in range(3)]
                    square = CORE_SQUARE + off[0] * off[0] + off[1] * off[1] + off[2] * off[2]
                    inverse = lax.rsqrt(square)
                    weight = numer[o, part, pl.ds(width * r, width)] * inverse * (inverse * inverse)
                    terms = [weight * off[c] for c in range(3)]
                    total = terms if total is None else [total[c] + terms[c] for c in range(3)]
                for c in range(3):
                    acc[o, c, part, :] = total[c]

    def velocity_of(position):
        high, low = split(acc[...].reshape(used * width, width))
        lane_sums = jnp.dot(
            jnp.concatenate([high, low], axis=1),
            jnp.ones((2 * width, width), jnp.bfloat16),
            preferred_element_type=jnp.float32,
        ).reshape(used, width, width)
        sums = [
            jnp.sum(jnp.where(diagonal, lane_sums[row], 0.0), axis=0, keepdims=True) for row in range(used)
        ]
        pair = jnp.concatenate(sums + [zeros], axis=0)
        before = jnp.where(lane == 0, position, pltpu.roll(position, 1, 1))
        after = jnp.where(lane == width - 1, position, pltpu.roll(position, width - 1, 1))
        chain = before + after - 2.0 * position
        force = COUPLE * pair + applied + TENSION * chain
        velocity = force / drag
        square = velocity * velocity
        tops = []
        for o in range(nb):
            tops.append(square[3 * o : 3 * o + 1] + square[3 * o + 1 : 3 * o + 2] + square[3 * o + 2 : 3 * o + 3])
        return velocity, functools.reduce(jnp.maximum, tops)

    def step_length(row):
        top = jnp.max(row, axis=1, keepdims=True)
        return STEP_LENGTH / (jnp.sqrt(top) + EPSILON)

    def next_slot(slot, numer, before):
        arrival = held.at[slot]
        pltpu.make_async_copy(arrival, arrival, state_recv.at[slot]).wait()
        fill_numer(slot, numer)
        add_slot(slot - 1, before, None)

    fill_numer(0, numer_even.at[0])
    acc[...] = jnp.zeros_like(acc)

    def two_slots(half, carry):
        next_slot(2 * half + 1, numer_odd.at[half], numer_even.at[half])
        next_slot(2 * half + 2, numer_even.at[half + 1], numer_odd.at[half])
        return carry

    halves = (slots - 1) // 2
    lax.fori_loop(0, halves, two_slots, 0)
    if slots % 2:
        add_slot(slots - 1, numer_even.at[halves], None)
    else:
        next_slot(lax.convert_element_type(dom * 0 + slots - 1, jnp.int32), numer_odd.at[halves], numer_even.at[halves])
        add_slot(slots - 1, numer_odd.at[halves], None)
    velocity, top = velocity_of(position)
    vel_tx[...] = jnp.concatenate([velocity[0 : 3 * nb], top, zeros[: spare - 1]], axis=0)
    top1_tx[...] = top

    def vel_copy(slot, target):
        return pltpu.make_async_remote_copy(
            src_ref=vel_tx,
            dst_ref=vel_rx.at[slot],
            send_sem=vel_send,
            recv_sem=vel_recv,
            device_id=target,
            device_id_type=MESH,
        )

    def top1_copy(index):
        kd, ks = index // (n_sub - 1) + 1, index % (n_sub - 1) + 1
        return pltpu.make_async_remote_copy(
            src_ref=top1_tx,
            dst_ref=top1_rx.at[index],
            send_sem=top1_send,
            recv_sem=top1_recv,
            device_id=(lax.rem(dom + kd, n_dom), lax.rem(sub + ks, n_sub)),
            device_id_type=MESH,
        )

    others = (n_sub - 1) * (n_dom - 1)
    repeat(1, n_dom, lambda k: vel_copy(n_sub - 1 + k, dom_at(k)).start())
    repeat(0, others, lambda k: top1_copy(k).start())
    repeat(1, n_sub, lambda k: vel_copy(k, sub_at(k)).start())

    vel_rx[0] = vel_tx[...]
    turned = velocity.T
    for o in range(nb):
        for c in range(3):
            vel_i[o, c] = jnp.broadcast_to(turned[:, 3 * o + c : 3 * o + c + 1], (width, width))

    arrived = vel_rx.at[pl.ds(1, slots - 1)]
    pltpu.make_async_copy(arrived, arrived, vel_recv).wait()
    pltpu.make_async_copy(top1_rx, top1_rx, top1_recv).wait()
    near = jnp.max(vel_rx[:, 3 * nb : 3 * nb + 1, :], axis=0)
    far = jnp.max(top1_rx[...], axis=0)
    step = step_length(jnp.maximum(near, far))

    position = position + step * velocity
    for o in range(nb):
        for c in range(3):
            at_i[o, c] = at_i[o, c] + step * vel_i[o, c]
    add_slot(0, numer_even.at[0], step, first=True)

    def again(half, carry):
        add_slot(2 * half + 1, numer_odd.at[half], carry)
        add_slot(2 * half + 2, numer_even.at[half + 1], carry)
        return carry

    lax.fori_loop(0, halves, again, step)
    if slots % 2 == 0:
        add_slot(slots - 1, numer_odd.at[halves], step)
    velocity, top = velocity_of(position)
    top2_tx[...] = top

    def top2_copy(index):
        kd, ks = (index + 1) // n_sub, (index + 1) % n_sub
        return pltpu.make_async_remote_copy(
            src_ref=top2_tx,
            dst_ref=top2_rx.at[index],
            send_sem=top2_send,
            recv_sem=top2_recv,
            device_id=(lax.rem(dom + kd, n_dom), lax.rem(sub + ks, n_sub)),
            device_id_type=MESH,
        )

    repeat(0, n_sub * n_dom - 1, lambda k: top2_copy(k).start())
    for o in range(nb):
        vel_ref[o] = velocity[3 * o : 3 * o + 3]

    repeat(1, n_sub, lambda k: sub_copy(k).wait_send())
    repeat(1, n_dom, lambda k: dom_copy(k).wait_send())
    pltpu.make_async_copy(arrived, arrived, vel_send).wait()
    pltpu.make_async_copy(top1_rx, top1_rx, top1_send).wait()

    pltpu.make_async_copy(top2_rx, top2_rx, top2_recv).wait()
    step = step_length(jnp.maximum(jnp.max(top2_rx[...], axis=0), top))
    position = position + step * velocity
    for o in range(nb):
        pos_ref[o] = position[3 * o : 3 * o + 3]
    pltpu.make_async_copy(top2_rx, top2_rx, top2_send).wait()


def solution(mesh):
    n_dom, n_sub = mesh.shape["dom"], mesh.shape["sub"]

    def local(segments, stress, drag_coef, send_ids, partner_ids):
        nb, _, width = segments.shape
        slots = n_sub + n_dom - 1
        f32 = jnp.float32
        vmem = pl.BlockSpec(memory_space=pltpu.VMEM)
        smem = pl.BlockSpec(memory_space=pltpu.SMEM)
        out = jax.ShapeDtypeStruct((nb, 3, width), f32)
        rows = 9 * nb + 2
        words = slots * nb * width * nb * width + (n_dom + slots) * (rows + 8) * width + 9 * nb * width * width
        return pl.pallas_call(
            functools.partial(kernel, n_dom, n_sub),
            out_shape=(out, out),
            in_specs=[vmem, vmem, smem, smem, smem],
            out_specs=(vmem, vmem),
            scratch_shapes=[
                pltpu.VMEM((n_dom, rows, width), f32),
                pltpu.VMEM((slots, rows, width), f32),
                pltpu.VMEM(((slots + 1) // 2, nb, width, nb * width), f32),
                pltpu.VMEM((slots // 2, nb, width, nb * width), f32),
                pltpu.VMEM((nb, width, DEPTH), jnp.bfloat16),
                pltpu.VMEM((nb, 3, width, width), f32),
                pltpu.VMEM((nb, 3, width, width), f32),
                pltpu.VMEM((nb, 3, width, width), f32),
                pltpu.VMEM((8, width), f32),
                pltpu.VMEM((slots, 8, width), f32),
                pltpu.VMEM((1, width), f32),
                pltpu.VMEM(((n_dom - 1) * (n_sub - 1), 1, width), f32),
                pltpu.VMEM((1, width), f32),
                pltpu.VMEM((n_dom * n_sub - 1, 1, width), f32),
                pltpu.SemaphoreType.DMA((slots,)),
                pltpu.SemaphoreType.DMA((slots,)),
                pltpu.SemaphoreType.DMA,
                pltpu.SemaphoreType.DMA,
                pltpu.SemaphoreType.DMA,
                pltpu.SemaphoreType.DMA,
                pltpu.SemaphoreType.DMA,
                pltpu.SemaphoreType.DMA,
            ],
            compiler_params=pltpu.CompilerParams(
                collective_id=0,
                has_side_effects=True,
                vmem_limit_bytes=4 * words + 8 * 1024 * 1024,
            ),
        )(
            segments,
            drag_coef,
            stress,
            send_ids.reshape(1, n_dom),
            partner_ids.reshape(1, n_dom),
        )

    in_specs = (
        P(("dom", "sub"), None, None),
        P(),
        P(("dom", "sub"), None),
        P(("dom", "sub"), None, None),
        P(("dom", "sub"), None, None),
    )
    out_specs = (P(("dom", "sub"), None, None), P(("dom", "sub"), None, None))
    return jax.shard_map(local, mesh=mesh, in_specs=in_specs, out_specs=out_specs, check_vma=False)
```

```python
import functools

import jax
import jax.numpy as jnp
from jax import lax
from jax.experimental import pallas as pl
from jax.experimental.pallas import tpu as pltpu
from jax.sharding import PartitionSpec as P

STEPS = 2
COUPLE = 0.0625
CORE_SQUARE = 0.5
TENSION = 0.25
STEP_LENGTH = 1.0
EPSILON = 1e-06

MESH = pl.DeviceIdType.MESH
DEPTH = 80
UNROLL_LIMIT = 64


def repeat(first, last, body):
    if last - first <= UNROLL_LIMIT:
        for index in range(first, last):
            body(index)
    else:

        def step(index, carry):
            body(index)
            return carry

        lax.fori_loop(first, last, step, 0)


def kernel(
    n_dom,
    n_sub,
    seg_ref,
    drag_ref,
    stress_ref,
    send_ref,
    partner_ref,
    pos_ref,
    vel_ref,
    stage,
    held,
    numer,
    left_side,
    at_i,
    vel_i,
    acc,
    vel_tx,
    vel_rx,
    top_tx,
    top_rx,
    state_send,
    state_recv,
    vel_send,
    vel_recv,
    top_send,
    top_recv,
):
    nb, _, width = seg_ref.shape
    slots = n_sub + n_dom - 1
    dom = lax.axis_index("dom")
    sub = lax.axis_index("sub")

    def sub_at(k):
        return (dom, lax.rem(sub + k, n_sub))

    def dom_at(k):
        return (lax.rem(dom + k, n_dom), sub)

    barrier = pltpu.get_barrier_semaphore()

    def greet_sub(k):
        pl.semaphore_signal(barrier, inc=1, device_id=sub_at(k), device_id_type=MESH)

    def greet_dom(k):
        pl.semaphore_signal(barrier, inc=1, device_id=dom_at(k), device_id_type=MESH)

    repeat(1, n_sub, greet_sub)
    repeat(1, n_dom, greet_dom)

    used = 3 * nb
    srow, prow, brow, lrow = used, used + 1, used + 2, 2 * used + 2
    for r in range(nb):
        for first, source in ((0, 0), (brow, 6), (lrow, 3)):
            held[0, first + 3 * r : first + 3 * r + 3, :] = seg_ref[r, source : source + 3, :]
    held[0, srow : prow + 1, :] = jnp.full((2, width), -1.0, jnp.float32)
    whole = held[0]
    row_id = lax.broadcasted_iota(jnp.int32, whole.shape, 0)
    stage[n_dom] = whole

    def fill(q):
        sent = send_ref[0, q].astype(jnp.float32)
        partner = partner_ref[0, q].astype(jnp.float32)
        stage[q] = jnp.where(row_id == srow, sent, jnp.where(row_id == prow, partner, whole))

    repeat(0, n_dom, fill)
    held[0] = stage[dom]

    def sub_copy(k):
        return pltpu.make_async_remote_copy(
            src_ref=stage.at[n_dom],
            dst_ref=held.at[k],
            send_sem=state_send.at[k],
            recv_sem=state_recv.at[k],
            device_id=sub_at(k),
            device_id_type=MESH,
        )

    def dom_copy(k):
        slot = n_sub - 1 + k
        return pltpu.make_async_remote_copy(
            src_ref=stage.at[lax.rem(dom + k, n_dom)],
            dst_ref=held.at[slot],
            send_sem=state_send.at[slot],
            recv_sem=state_recv.at[slot],
            device_id=dom_at(k),
            device_id_type=MESH,
        )

    pl.semaphore_wait(barrier, slots - 1)
    repeat(1, n_dom, lambda k: dom_copy(k).start())
    repeat(1, n_sub, lambda k: sub_copy(k).start())

    applied_rows = []
    drag_rows = []
    for o in range(nb):
        b = [seg_ref[o, 6 + c : 7 + c, :] for c in range(3)]
        ln = [seg_ref[o, 3 + c : 4 + c, :] for c in range(3)]
        pulled = [
            stress_ref[c, 0] * b[0] + stress_ref[c, 1] * b[1] + stress_ref[c, 2] * b[2] for c in range(3)
        ]
        applied_rows.append(pulled[1] * ln[2] - pulled[2] * ln[1])
        applied_rows.append(pulled[2] * ln[0] - pulled[0] * ln[2])
        applied_rows.append(pulled[0] * ln[1] - pulled[1] * ln[0])
        drag_rows.extend([drag_ref[o : o + 1, :]] * 3)
    spare = 8 - 3 * nb
    zeros = jnp.zeros((spare, width), jnp.float32)
    applied = jnp.concatenate(applied_rows + [zeros], axis=0)
    drag = jnp.concatenate(drag_rows + [zeros + 1.0], axis=0)
    position = jnp.concatenate([seg_ref[o, 0:3, :] for o in range(nb)] + [zeros], axis=0)
    lane = lax.broadcasted_iota(jnp.int32, (8, width), 1)
    tile_row = lax.broadcasted_iota(jnp.int32, (8, width), 0)
    diagonal = lax.broadcasted_iota(jnp.int32, (width, width), 0) == lax.broadcasted_iota(
        jnp.int32, (width, width), 1
    )

    def split(value):
        high = value.astype(jnp.bfloat16)
        low = (value - high.astype(jnp.float32)).astype(jnp.bfloat16)
        return high, low

    for o in range(nb):
        lines = jnp.concatenate([seg_ref[o, 3:6, :]] * nb + [zeros], axis=0)
        product = jnp.concatenate([seg_ref[o, 6 + a : 7 + a, :] * lines for a in range(3)], axis=0)
        high = product.astype(jnp.bfloat16).astype(jnp.float32)
        rest = jnp.zeros((DEPTH - 72, width), jnp.float32)
        left_side[o] = jnp.concatenate([high, high, product - high, rest], axis=0).T.astype(jnp.bfloat16)
    turned = position.T
    for o in range(nb):
        for c in range(3):
            at_i[o, c] = jnp.broadcast_to(turned[:, 3 * o + c : 3 * o + c + 1], (width, width))

    def fill_numer(where):
        base = jnp.full((1, width), jnp.where(where < n_sub, 1.0, 0.0), jnp.float32)
        in_column = where >= n_sub
        peer = jnp.where(in_column, lax.rem(dom - where + n_sub - 1 + n_dom, n_dom), dom)
        listed = jnp.logical_or(in_column, where == 0)
        sent = jnp.where(listed, send_ref[0, peer], -1)
        partner = partner_ref[0, peer]
        got, for_mine = held[where, srow : srow + 1, :], held[where, prow : prow + 1, :]
        table = []
        for o in range(nb):
            row = []
            for r in range(nb):
                mine = jnp.logical_and(sent == o, partner == r)
                theirs = jnp.logical_and(got == float(r), for_mine == float(o))
                row.append(base + jnp.where(mine, 1.0, 0.0) + jnp.where(theirs, 1.0, 0.0))
            table.append(row)
        lines = jnp.concatenate([held[where, lrow : lrow + used, :], zeros], axis=0)
        pieces = []
        for r in range(nb):
            here = jnp.logical_and(tile_row >= 3 * r, tile_row < 3 * r + 3)
            own_lines = jnp.where(here, lines, 0.0)
            b = [held[where, brow + 3 * r + a : brow + 3 * r + a + 1, :] for a in range(3)]
            pieces.append(jnp.concatenate([b[a] * own_lines for a in range(3)], axis=0))
        for o in range(nb):
            right = jnp.concatenate([pieces[r] * table[o][r] for r in range(nb)], axis=1)
            high = right.astype(jnp.bfloat16).astype(jnp.float32)
            rest = jnp.zeros((DEPTH - 72, nb * width), jnp.float32)
            stack = jnp.concatenate([high, right - high, high, rest], axis=0)
            numer[where, o] = jnp.dot(
                left_side[o], stack.astype(jnp.bfloat16), preferred_element_type=jnp.float32
            )

    def add_slot(slot):
        rows = []
        for r in range(nb):
            for c in range(3):
                row = held[slot, 3 * r + c : 3 * r + c + 1, :]
                rows.append(jnp.broadcast_to(row, (8, width)))
        for o in range(nb):
            for g in range(width // 8):
                part = pl.ds(8 * g, 8)
                mine = [at_i[o, c, part, :] for c in range(3)]
                total = [acc[o, c, part, :] for c in range(3)]
                for r in range(nb):
                    off = [mine[c] - rows[r * 3 + c] for c in range(3)]
                    square = CORE_SQUARE + off[0] * off[0] + off[1] * off[1] + off[2] * off[2]
                    inverse = lax.rsqrt(square)
                    weight = numer[slot, o, part, pl.ds(width * r, width)] * inverse * (inverse * inverse)
                    terms = [weight * off[c] for c in range(3)]
                    total = [total[c] + terms[c] for c in range(3)]
                for c in range(3):
                    acc[o, c, part, :] = total[c]

    def velocity_of(position):
        high, low = split(acc[...].reshape(used * width, width))
        lane_sums = jnp.dot(
            jnp.concatenate([high, low], axis=1),
            jnp.ones((2 * width, width), jnp.bfloat16),
            preferred_element_type=jnp.float32,
        ).reshape(used, width, width)
        sums = [
            jnp.sum(jnp.where(diagonal, lane_sums[row], 0.0), axis=0, keepdims=True) for row in range(used)
        ]
        pair = jnp.concatenate(sums + [zeros], axis=0)
        before = jnp.where(lane == 0, position, pltpu.roll(position, 1, 1))
        after = jnp.where(lane == width - 1, position, pltpu.roll(position, width - 1, 1))
        chain = before + after - 2.0 * position
        force = COUPLE * pair + applied + TENSION * chain
        velocity = force / drag
        square = velocity * velocity
        tops = []
        for o in range(nb):
            tops.append(square[3 * o : 3 * o + 1] + square[3 * o + 1 : 3 * o + 2] + square[3 * o + 2 : 3 * o + 3])
        return velocity, functools.reduce(jnp.maximum, tops)

    def step_length(row):
        top = jnp.max(row, axis=1, keepdims=True)
        return STEP_LENGTH / (jnp.sqrt(top) + EPSILON)

    def vel_copy(slot, device):
        return pltpu.make_async_remote_copy(
            src_ref=vel_tx,
            dst_ref=vel_rx.at[slot],
            send_sem=vel_send,
            recv_sem=vel_recv,
            device_id=device,
            device_id_type=MESH,
        )

    arrived = vel_rx.at[pl.ds(1, slots - 1)]

    def one_step(index, carry):
        position, _ = carry
        acc[...] = jnp.zeros_like(acc)

        def one_slot(slot, inner):
            @pl.when(index == 0)
            def _():
                @pl.when(slot > 0)
                def _():
                    arrival = held.at[slot]
                    pltpu.make_async_copy(arrival, arrival, state_recv.at[slot]).wait()

                fill_numer(slot)

            add_slot(slot)
            return inner

        lax.fori_loop(0, slots, one_slot, 0)
        velocity, top = velocity_of(position)
        top_tx[index] = top

        def top_copy(place):
            kd, ks = (place + 1) // n_sub, (place + 1) % n_sub
            return pltpu.make_async_remote_copy(
                src_ref=top_tx.at[index],
                dst_ref=top_rx.at[index, place],
                send_sem=top_send.at[index],
                recv_sem=top_recv.at[index],
                device_id=(lax.rem(dom + kd, n_dom), lax.rem(sub + ks, n_sub)),
                device_id_type=MESH,
            )

        @pl.when(index == 0)
        def _():
            vel_tx[...] = velocity
            repeat(1, n_dom, lambda k: vel_copy(n_sub - 1 + k, dom_at(k)).start())
            repeat(1, n_sub, lambda k: vel_copy(k, sub_at(k)).start())

        repeat(0, n_sub * n_dom - 1, lambda k: top_copy(k).start())

        @pl.when(index == 0)
        def _():
            vel_rx[0] = velocity
            turned = velocity.T
            for o in range(nb):
                for c in range(3):
                    vel_i[o, c] = jnp.broadcast_to(turned[:, 3 * o + c : 3 * o + c + 1], (width, width))
            pltpu.make_async_copy(arrived, arrived, vel_recv).wait()

        tops = top_rx.at[index]
        pltpu.make_async_copy(tops, tops, top_recv.at[index]).wait()
        step = step_length(jnp.maximum(jnp.max(top_rx[index], axis=0), top))

        @pl.when(index == 0)
        def _():
            at_i[...] = at_i[...] + step * vel_i[...]
            held[:, 0:8, :] = held[:, 0:8, :] + step * vel_rx[...]

        return position + step * velocity, velocity

    position, velocity = lax.fori_loop(0, STEPS, one_step, (position, jnp.zeros_like(position)))
    for o in range(nb):
        vel_ref[o] = velocity[3 * o : 3 * o + 3]
        pos_ref[o] = position[3 * o : 3 * o + 3]

    repeat(1, n_sub, lambda k: sub_copy(k).wait_send())
    repeat(1, n_dom, lambda k: dom_copy(k).wait_send())
    pltpu.make_async_copy(arrived, arrived, vel_send).wait()
    for index in range(STEPS):
        tops = top_rx.at[index]
        pltpu.make_async_copy(tops, tops, top_send.at[index]).wait()


def solution(mesh):
    n_dom, n_sub = mesh.shape["dom"], mesh.shape["sub"]

    def local(segments, stress, drag_coef, send_ids, partner_ids):
        nb, _, width = segments.shape
        slots = n_sub + n_dom - 1
        f32 = jnp.float32
        vmem = pl.BlockSpec(memory_space=pltpu.VMEM)
        smem = pl.BlockSpec(memory_space=pltpu.SMEM)
        out = jax.ShapeDtypeStruct((nb, 3, width), f32)
        rows = 9 * nb + 2
        words = 2 * STEPS * n_dom * n_sub * width + slots * nb * width * nb * width + (n_dom + slots) * (rows + 8) * width + 9 * nb * width * width
        return pl.pallas_call(
            functools.partial(kernel, n_dom, n_sub),
            out_shape=(out, out),
            in_specs=[vmem, vmem, smem, smem, smem],
            out_specs=(vmem, vmem),
            scratch_shapes=[
                pltpu.VMEM((n_dom + 1, rows, width), f32),
                pltpu.VMEM((slots, rows, width), f32),
                pltpu.VMEM((slots, nb, width, nb * width), f32),
                pltpu.VMEM((nb, width, DEPTH), jnp.bfloat16),
                pltpu.VMEM((nb, 3, width, width), f32),
                pltpu.VMEM((nb, 3, width, width), f32),
                pltpu.VMEM((nb, 3, width, width), f32),
                pltpu.VMEM((8, width), f32),
                pltpu.VMEM((slots, 8, width), f32),
                pltpu.VMEM((STEPS, 1, width), f32),
                pltpu.VMEM((STEPS, n_dom * n_sub - 1, 1, width), f32),
                pltpu.SemaphoreType.DMA((slots,)),
                pltpu.SemaphoreType.DMA((slots,)),
                pltpu.SemaphoreType.DMA,
                pltpu.SemaphoreType.DMA,
                pltpu.SemaphoreType.DMA((STEPS,)),
                pltpu.SemaphoreType.DMA((STEPS,)),
            ],
            compiler_params=pltpu.CompilerParams(
                collective_id=0,
                has_side_effects=True,
                vmem_limit_bytes=4 * words + 8 * 1024 * 1024,
            ),
        )(
            segments,
            drag_coef,
            stress,
            send_ids.reshape(1, n_dom),
            partner_ids.reshape(1, n_dom),
        )

    in_specs = (
        P(("dom", "sub"), None, None),
        P(),
        P(("dom", "sub"), None),
        P(("dom", "sub"), None, None),
        P(("dom", "sub"), None, None),
    )
    out_specs = (P(("dom", "sub"), None, None), P(("dom", "sub"), None, None))
    return jax.shard_map(local, mesh=mesh, in_specs=in_specs, out_specs=out_specs, check_vma=False)
```

```python
import functools

import jax
import jax.numpy as jnp
from jax import lax
from jax.experimental import pallas as pl
from jax.experimental.pallas import tpu as pltpu
from jax.sharding import PartitionSpec as P

STEPS = 2
COUPLE = 0.0625
CORE_SQUARE = 0.5
TENSION = 0.25
STEP_LENGTH = 1.0
EPSILON = 1e-06

MESH = pl.DeviceIdType.MESH
DEPTH = 80
UNROLL_LIMIT = 64


def repeat(first, last, body):
    if last - first <= UNROLL_LIMIT:
        for index in range(first, last):
            body(index)
    else:

        def step(index, carry):
            body(index)
            return carry

        lax.fori_loop(first, last, step, 0)


def kernel(
    n_dom,
    n_sub,
    seg_ref,
    drag_ref,
    stress_ref,
    send_ref,
    partner_ref,
    pos_ref,
    vel_ref,
    stage,
    held,
    numer,
    left_side,
    at_i,
    vel_i,
    acc,
    sources,
    vel_tx,
    vel_rx,
    top1_tx,
    top1_rx,
    top2_tx,
    top2_rx,
    state_send,
    state_recv,
    vel_send,
    vel_recv,
    top1_send,
    top1_recv,
    top2_send,
    top2_recv,
):
    nb, _, width = seg_ref.shape
    slots = n_sub + n_dom - 1
    dom = lax.axis_index("dom")
    sub = lax.axis_index("sub")

    def sub_at(k):
        return (dom, lax.rem(sub + k, n_sub))

    def dom_at(k):
        return (lax.rem(dom + k, n_dom), sub)

    barrier = pltpu.get_barrier_semaphore()

    def greet_sub(k):
        pl.semaphore_signal(barrier, inc=1, device_id=sub_at(k), device_id_type=MESH)

    def greet_dom(k):
        pl.semaphore_signal(barrier, inc=1, device_id=dom_at(k), device_id_type=MESH)

    repeat(1, n_sub, greet_sub)
    repeat(1, n_dom, greet_dom)

    used = 3 * nb
    srow, prow, brow, lrow = used, used + 1, used + 2, 2 * used + 2
    for r in range(nb):
        for first, source in ((0, 0), (brow, 6), (lrow, 3)):
            held[0, first + 3 * r : first + 3 * r + 3, :] = seg_ref[r, source : source + 3, :]
    held[0, srow : prow + 1, :] = jnp.zeros((2, width), jnp.float32)
    whole = held[0]
    row_id = lax.broadcasted_iota(jnp.int32, whole.shape, 0)

    def fill(q):
        sent = send_ref[0, q].astype(jnp.float32)
        partner = partner_ref[0, q].astype(jnp.float32)
        stage[q] = jnp.where(row_id == srow, sent, jnp.where(row_id == prow, partner, whole))

    repeat(0, n_dom, fill)

    def sub_copy(k):
        return pltpu.make_async_remote_copy(
            src_ref=held.at[0],
            dst_ref=held.at[k],
            send_sem=state_send.at[k],
            recv_sem=state_recv.at[k],
            device_id=sub_at(k),
            device_id_type=MESH,
        )

    def dom_copy(k):
        slot = n_sub - 1 + k
        return pltpu.make_async_remote_copy(
            src_ref=stage.at[lax.rem(dom + k, n_dom)],
            dst_ref=held.at[slot],
            send_sem=state_send.at[slot],
            recv_sem=state_recv.at[slot],
            device_id=dom_at(k),
            device_id_type=MESH,
        )

    pl.semaphore_wait(barrier, slots - 1)
    repeat(1, n_dom, lambda k: dom_copy(k).start())
    repeat(1, n_sub, lambda k: sub_copy(k).start())

    applied_rows = []
    drag_rows = []
    for o in range(nb):
        b = [seg_ref[o, 6 + c : 7 + c, :] for c in range(3)]
        ln = [seg_ref[o, 3 + c : 4 + c, :] for c in range(3)]
        pulled = [
            stress_ref[c, 0] * b[0] + stress_ref[c, 1] * b[1] + stress_ref[c, 2] * b[2] for c in range(3)
        ]
        applied_rows.append(pulled[1] * ln[2] - pulled[2] * ln[1])
        applied_rows.append(pulled[2] * ln[0] - pulled[0] * ln[2])
        applied_rows.append(pulled[0] * ln[1] - pulled[1] * ln[0])
        drag_rows.extend([drag_ref[o : o + 1, :]] * 3)
    spare = 8 - 3 * nb
    zeros = jnp.zeros((spare, width), jnp.float32)
    applied = jnp.concatenate(applied_rows + [zeros], axis=0)
    drag = jnp.concatenate(drag_rows + [zeros + 1.0], axis=0)
    position = jnp.concatenate([seg_ref[o, 0:3, :] for o in range(nb)] + [zeros], axis=0)
    lane = lax.broadcasted_iota(jnp.int32, (8, width), 1)
    tile_row = lax.broadcasted_iota(jnp.int32, (8, width), 0)
    diagonal = lax.broadcasted_iota(jnp.int32, (width, width), 0) == lax.broadcasted_iota(
        jnp.int32, (width, width), 1
    )

    def split(value):
        high = value.astype(jnp.bfloat16)
        low = (value - high.astype(jnp.float32)).astype(jnp.bfloat16)
        return high, low

    for o in range(nb):
        lines = jnp.concatenate([seg_ref[o, 3:6, :]] * nb + [zeros], axis=0)
        product = jnp.concatenate([seg_ref[o, 6 + a : 7 + a, :] * lines for a in range(3)], axis=0)
        high = product.astype(jnp.bfloat16).astype(jnp.float32)
        rest = jnp.zeros((DEPTH - 72, width), jnp.float32)
        left_side[o] = jnp.concatenate([high, high, product - high, rest], axis=0).T.astype(jnp.bfloat16)
    turned = position.T
    for o in range(nb):
        for c in range(3):
            at_i[o, c] = jnp.broadcast_to(turned[:, 3 * o + c : 3 * o + c + 1], (width, width))

    def counts(slot, base, peer):
        table = []
        for o in range(nb):
            row = []
            for r in range(nb):
                value = jnp.full((1, width), base, jnp.float32)
                if peer is not None:
                    sent, partner = send_ref[0, peer], partner_ref[0, peer]
                    mine = jnp.logical_and(sent == o, partner == r)
                    value = value + jnp.where(mine, 1.0, 0.0)
                    source = stage if slot is None else held
                    place = dom if slot is None else slot
                    got, for_mine = source[place, srow : srow + 1, :], source[place, prow : prow + 1, :]
                    value = value + jnp.where(
                        jnp.logical_and(got == float(r), for_mine == float(o)), 1.0, 0.0
                    )
                row.append(value)
            table.append(row)
        return table

    def fill_numer(slot, base, peer):
        where = 0 if slot is None else slot
        table = counts(slot, base, peer)
        lines = jnp.concatenate([held[where, lrow : lrow + used, :], zeros], axis=0)
        pieces = []
        for r in range(nb):
            here = jnp.logical_and(tile_row >= 3 * r, tile_row < 3 * r + 3)
            own_lines = jnp.where(here, lines, 0.0)
            b = [held[where, brow + 3 * r + a : brow + 3 * r + a + 1, :] for a in range(3)]
            pieces.append(jnp.concatenate([b[a] * own_lines for a in range(3)], axis=0))
        for o in range(nb):
            right = jnp.concatenate([pieces[r] * table[o][r] for r in range(nb)], axis=1)
            high = right.astype(jnp.bfloat16).astype(jnp.float32)
            rest = jnp.zeros((DEPTH - 72, nb * width), jnp.float32)
            stack = jnp.concatenate([high, right - high, high, rest], axis=0)
            numer[where, o] = jnp.dot(
                left_side[o], stack.astype(jnp.bfloat16), preferred_element_type=jnp.float32
            )

    def add_slot(slot, step, first=False):
        rows = []
        for r in range(nb):
            for c in range(3):
                row = held[slot, 3 * r + c : 3 * r + c + 1, :]
                if step is not None:
                    row = row + step * vel_rx[slot, r * 3 + c : r * 3 + c + 1, :]
                rows.append(jnp.broadcast_to(row, (8, width)))
        for o in range(nb):
            for g in range(width // 8):
                part = pl.ds(8 * g, 8)
                mine = [at_i[o, c, part, :] for c in range(3)]
                total = None if first else [acc[o, c, part, :] for c in range(3)]
                for r in range(nb):
                    off = [mine[c] - rows[r * 3 + c] for c in range(3)]
                    square = CORE_SQUARE + off[0] * off[0] + off[1] * off[1] + off[2] * off[2]
                    inverse = lax.rsqrt(square)
                    weight = numer[slot, o, part, pl.ds(width * r, width)] * inverse * (inverse * inverse)
                    terms = [weight * off[c] for c in range(3)]
                    total = terms if total is None else [total[c] + terms[c] for c in range(3)]
                for c in range(3):
                    acc[o, c, part, :] = total[c]

    def velocity_of(position):
        high, low = split(acc[...].reshape(used * width, width))
        lane_sums = jnp.dot(
            jnp.concatenate([high, low], axis=1),
            jnp.ones((2 * width, width), jnp.bfloat16),
            preferred_element_type=jnp.float32,
        ).reshape(used, width, width)
        sums = [
            jnp.sum(jnp.where(diagonal, lane_sums[row], 0.0), axis=0, keepdims=True) for row in range(used)
        ]
        pair = jnp.concatenate(sums + [zeros], axis=0)
        before = jnp.where(lane == 0, position, pltpu.roll(position, 1, 1))
        after = jnp.where(lane == width - 1, position, pltpu.roll(position, width - 1, 1))
        chain = before + after - 2.0 * position
        force = COUPLE * pair + applied + TENSION * chain
        velocity = force / drag
        square = velocity * velocity
        tops = []
        for o in range(nb):
            tops.append(square[3 * o : 3 * o + 1] + square[3 * o + 1 : 3 * o + 2] + square[3 * o + 2 : 3 * o + 3])
        return velocity, functools.reduce(jnp.maximum, tops)

    def step_length(row):
        top = jnp.max(row, axis=1, keepdims=True)
        return STEP_LENGTH / (jnp.sqrt(top) + EPSILON)

    fill_numer(None, 1.0, dom)
    add_slot(0, None, first=True)

    def from_sub(k, carry):
        sub_copy(k).wait_recv()
        fill_numer(k, 1.0, None)
        add_slot(k, None)
        return carry

    def from_dom(k, carry):
        slot = n_sub - 1 + k
        dom_copy(k).wait_recv()
        fill_numer(slot, 0.0, lax.rem(dom - k + n_dom, n_dom))
        add_slot(slot, None)
        return carry

    lax.fori_loop(1, n_sub, from_sub, 0)
    lax.fori_loop(1, n_dom, from_dom, 0)
    velocity, top = velocity_of(position)
    vel_tx[...] = jnp.concatenate([velocity[0 : 3 * nb], top, zeros[: spare - 1]], axis=0)
    top1_tx[...] = top

    def vel_copy(slot, target):
        return pltpu.make_async_remote_copy(
            src_ref=vel_tx,
            dst_ref=vel_rx.at[slot],
            send_sem=vel_send,
            recv_sem=vel_recv,
            device_id=target,
            device_id_type=MESH,
        )

    def top1_copy(index):
        kd, ks = index // (n_sub - 1) + 1, index % (n_sub - 1) + 1
        return pltpu.make_async_remote_copy(
            src_ref=top1_tx,
            dst_ref=top1_rx.at[index],
            send_sem=top1_send,
            recv_sem=top1_recv,
            device_id=(lax.rem(dom + kd, n_dom), lax.rem(sub + ks, n_sub)),
            device_id_type=MESH,
        )

    others = (n_sub - 1) * (n_dom - 1)
    repeat(1, n_dom, lambda k: vel_copy(n_sub - 1 + k, dom_at(k)).start())
    repeat(0, others, lambda k: top1_copy(k).start())
    repeat(1, n_sub, lambda k: vel_copy(k, sub_at(k)).start())

    vel_rx[0] = vel_tx[...]
    turned = velocity.T
    for o in range(nb):
        for c in range(3):
            vel_i[o, c] = jnp.broadcast_to(turned[:, 3 * o + c : 3 * o + c + 1], (width, width))

    arrived = vel_rx.at[pl.ds(1, slots - 1)]
    pltpu.make_async_copy(arrived, arrived, vel_recv).wait()
    pltpu.make_async_copy(top1_rx, top1_rx, top1_recv).wait()
    near = jnp.max(vel_rx[:, 3 * nb : 3 * nb + 1, :], axis=0)
    far = jnp.max(top1_rx[...], axis=0)
    step = step_length(jnp.maximum(near, far))

    position = position + step * velocity

    def move(slot):
        tile = held[slot, 0:8, :] + step * vel_rx[slot]
        for row in range(used):
            sources[slot, row] = jnp.broadcast_to(tile[row : row + 1], (8, width))

    repeat(0, slots, move)

    def chunk(g, carry):
        part = pl.ds(pl.multiple_of(8 * g, 8), 8)
        mine = [[at_i[o, c, part, :] + step * vel_i[o, c, part, :] for c in range(3)] for o in range(nb)]

        def add_one(slot, total):
            total = list(total)
            for r in range(nb):
                theirs = [sources[slot, 3 * r + c] for c in range(3)]
                for o in range(nb):
                    off = [mine[o][c] - theirs[c] for c in range(3)]
                    square = CORE_SQUARE + off[0] * off[0] + off[1] * off[1] + off[2] * off[2]
                    inverse = lax.rsqrt(square)
                    weight = numer[slot, o, part, pl.ds(width * r, width)] * inverse * (inverse * inverse)
                    for c in range(3):
                        total[3 * o + c] = total[3 * o + c] + weight * off[c]
            return total

        total = [jnp.zeros((8, width), jnp.float32)] * used
        if slots <= UNROLL_LIMIT:
            for slot in range(slots):
                total = add_one(slot, total)
        else:
            total = lax.fori_loop(0, slots, add_one, total)
        for o in range(nb):
            for c in range(3):
                acc[o, c, part, :] = total[3 * o + c]
        return carry

    lax.fori_loop(0, width // 8, chunk, 0, unroll=4)
    velocity, top = velocity_of(position)
    top2_tx[...] = top

    def top2_copy(index):
        kd, ks = (index + 1) // n_sub, (index + 1) % n_sub
        return pltpu.make_async_remote_copy(
            src_ref=top2_tx,
            dst_ref=top2_rx.at[index],
            send_sem=top2_send,
            recv_sem=top2_recv,
            device_id=(lax.rem(dom + kd, n_dom), lax.rem(sub + ks, n_sub)),
            device_id_type=MESH,
        )

    repeat(0, n_sub * n_dom - 1, lambda k: top2_copy(k).start())
    for o in range(nb):
        vel_ref[o] = velocity[3 * o : 3 * o + 3]

    repeat(1, n_sub, lambda k: sub_copy(k).wait_send())
    repeat(1, n_dom, lambda k: dom_copy(k).wait_send())
    pltpu.make_async_copy(arrived, arrived, vel_send).wait()
    pltpu.make_async_copy(top1_rx, top1_rx, top1_send).wait()

    pltpu.make_async_copy(top2_rx, top2_rx, top2_recv).wait()
    step = step_length(jnp.maximum(jnp.max(top2_rx[...], axis=0), top))
    position = position + step * velocity
    for o in range(nb):
        pos_ref[o] = position[3 * o : 3 * o + 3]
    pltpu.make_async_copy(top2_rx, top2_rx, top2_send).wait()


def solution(mesh):
    n_dom, n_sub = mesh.shape["dom"], mesh.shape["sub"]

    def local(segments, stress, drag_coef, send_ids, partner_ids):
        nb, _, width = segments.shape
        slots = n_sub + n_dom - 1
        f32 = jnp.float32
        vmem = pl.BlockSpec(memory_space=pltpu.VMEM)
        smem = pl.BlockSpec(memory_space=pltpu.SMEM)
        out = jax.ShapeDtypeStruct((nb, 3, width), f32)
        rows = 9 * nb + 2
        words = 48 * slots * width + slots * nb * width * nb * width + (n_dom + slots) * (rows + 8) * width + 9 * nb * width * width
        return pl.pallas_call(
            functools.partial(kernel, n_dom, n_sub),
            out_shape=(out, out),
            in_specs=[vmem, vmem, smem, smem, smem],
            out_specs=(vmem, vmem),
            scratch_shapes=[
                pltpu.VMEM((n_dom, rows, width), f32),
                pltpu.VMEM((slots, rows, width), f32),
                pltpu.VMEM((slots, nb, width, nb * width), f32),
                pltpu.VMEM((nb, width, DEPTH), jnp.bfloat16),
                pltpu.VMEM((nb, 3, width, width), f32),
                pltpu.VMEM((nb, 3, width, width), f32),
                pltpu.VMEM((nb, 3, width, width), f32),
                pltpu.VMEM((slots, 3 * nb, 8, width), f32),
                pltpu.VMEM((8, width), f32),
                pltpu.VMEM((slots, 8, width), f32),
                pltpu.VMEM((1, width), f32),
                pltpu.VMEM(((n_dom - 1) * (n_sub - 1), 1, width), f32),
                pltpu.VMEM((1, width), f32),
                pltpu.VMEM((n_dom * n_sub - 1, 1, width), f32),
                pltpu.SemaphoreType.DMA((slots,)),
                pltpu.SemaphoreType.DMA((slots,)),
                pltpu.SemaphoreType.DMA,
                pltpu.SemaphoreType.DMA,
                pltpu.SemaphoreType.DMA,
                pltpu.SemaphoreType.DMA,
                pltpu.SemaphoreType.DMA,
                pltpu.SemaphoreType.DMA,
            ],
            compiler_params=pltpu.CompilerParams(
                collective_id=0,
                has_side_effects=True,
                vmem_limit_bytes=4 * words + 8 * 1024 * 1024,
            ),
        )(
            segments,
            drag_coef,
            stress,
            send_ids.reshape(1, n_dom),
            partner_ids.reshape(1, n_dom),
        )

    in_specs = (
        P(("dom", "sub"), None, None),
        P(),
        P(("dom", "sub"), None),
        P(("dom", "sub"), None, None),
        P(("dom", "sub"), None, None),
    )
    out_specs = (P(("dom", "sub"), None, None), P(("dom", "sub"), None, None))
    return jax.shard_map(local, mesh=mesh, in_specs=in_specs, out_specs=out_specs, check_vma=False)
```

```python
import functools

import jax
import jax.numpy as jnp
from jax import lax
from jax.experimental import pallas as pl
from jax.experimental.pallas import tpu as pltpu
from jax.sharding import PartitionSpec as P

STEPS = 2
COUPLE = 0.0625
CORE_SQUARE = 0.5
TENSION = 0.25
STEP_LENGTH = 1.0
EPSILON = 1e-06

MESH = pl.DeviceIdType.MESH
DEPTH = 80
UNROLL_LIMIT = 64


def repeat(first, last, body):
    if last - first <= UNROLL_LIMIT:
        for index in range(first, last):
            body(index)
    else:

        def step(index, carry):
            body(index)
            return carry

        lax.fori_loop(first, last, step, 0)


def kernel(
    n_dom,
    n_sub,
    seg_ref,
    drag_ref,
    stress_ref,
    send_ref,
    partner_ref,
    pos_ref,
    vel_ref,
    stage,
    held,
    numer,
    left_side,
    at_i,
    vel_i,
    acc,
    sources,
    vel_tx,
    vel_rx,
    top1_tx,
    top1_rx,
    top2_tx,
    top2_rx,
    state_send,
    state_recv,
    vel_send,
    vel_recv,
    top1_send,
    top1_recv,
    top2_send,
    top2_recv,
):
    nb, _, width = seg_ref.shape
    slots = n_sub + n_dom - 1
    dom = lax.axis_index("dom")
    sub = lax.axis_index("sub")

    def sub_at(k):
        return (dom, lax.rem(sub + k, n_sub))

    def dom_at(k):
        return (lax.rem(dom + k, n_dom), sub)

    barrier = pltpu.get_barrier_semaphore()

    def greet_sub(k):
        pl.semaphore_signal(barrier, inc=1, device_id=sub_at(k), device_id_type=MESH)

    def greet_dom(k):
        pl.semaphore_signal(barrier, inc=1, device_id=dom_at(k), device_id_type=MESH)

    repeat(1, n_sub, greet_sub)
    repeat(1, n_dom, greet_dom)

    used = 3 * nb
    srow, prow, brow, lrow = used, used + 1, used + 2, 2 * used + 2
    for r in range(nb):
        for first, source in ((0, 0), (brow, 6), (lrow, 3)):
            held[0, first + 3 * r : first + 3 * r + 3, :] = seg_ref[r, source : source + 3, :]
    held[0, srow : prow + 1, :] = jnp.zeros((2, width), jnp.float32)
    whole = held[0]
    row_id = lax.broadcasted_iota(jnp.int32, whole.shape, 0)

    def fill(q):
        sent = send_ref[0, q].astype(jnp.float32)
        partner = partner_ref[0, q].astype(jnp.float32)
        stage[q] = jnp.where(row_id == srow, sent, jnp.where(row_id == prow, partner, whole))

    repeat(0, n_dom, fill)

    def sub_copy(k):
        return pltpu.make_async_remote_copy(
            src_ref=held.at[0],
            dst_ref=held.at[k],
            send_sem=state_send.at[k],
            recv_sem=state_recv.at[k],
            device_id=sub_at(k),
            device_id_type=MESH,
        )

    def dom_copy(k):
        slot = n_sub - 1 + k
        return pltpu.make_async_remote_copy(
            src_ref=stage.at[lax.rem(dom + k, n_dom)],
            dst_ref=held.at[slot],
            send_sem=state_send.at[slot],
            recv_sem=state_recv.at[slot],
            device_id=dom_at(k),
            device_id_type=MESH,
        )

    applied_rows = []
    drag_rows = []
    for o in range(nb):
        b = [seg_ref[o, 6 + c : 7 + c, :] for c in range(3)]
        ln = [seg_ref[o, 3 + c : 4 + c, :] for c in range(3)]
        pulled = [
            stress_ref[c, 0] * b[0] + stress_ref[c, 1] * b[1] + stress_ref[c, 2] * b[2] for c in range(3)
        ]
        applied_rows.append(pulled[1] * ln[2] - pulled[2] * ln[1])
        applied_rows.append(pulled[2] * ln[0] - pulled[0] * ln[2])
        applied_rows.append(pulled[0] * ln[1] - pulled[1] * ln[0])
        drag_rows.extend([drag_ref[o : o + 1, :]] * 3)
    spare = 8 - 3 * nb
    zeros = jnp.zeros((spare, width), jnp.float32)
    applied = jnp.concatenate(applied_rows + [zeros], axis=0)
    drag = jnp.concatenate(drag_rows + [zeros + 1.0], axis=0)
    position = jnp.concatenate([seg_ref[o, 0:3, :] for o in range(nb)] + [zeros], axis=0)
    lane = lax.broadcasted_iota(jnp.int32, (8, width), 1)
    tile_row = lax.broadcasted_iota(jnp.int32, (8, width), 0)
    diagonal = lax.broadcasted_iota(jnp.int32, (width, width), 0) == lax.broadcasted_iota(
        jnp.int32, (width, width), 1
    )

    def split(value):
        high = value.astype(jnp.bfloat16)
        low = (value - high.astype(jnp.float32)).astype(jnp.bfloat16)
        return high, low

    for o in range(nb):
        lines = jnp.concatenate([seg_ref[o, 3:6, :]] * nb + [zeros], axis=0)
        product = jnp.concatenate([seg_ref[o, 6 + a : 7 + a, :] * lines for a in range(3)], axis=0)
        high = product.astype(jnp.bfloat16).astype(jnp.float32)
        rest = jnp.zeros((DEPTH - 72, width), jnp.float32)
        left_side[o] = jnp.concatenate([high, high, product - high, rest], axis=0).T.astype(jnp.bfloat16)
    turned = position.T
    for o in range(nb):
        for c in range(3):
            at_i[o, c] = jnp.broadcast_to(turned[:, 3 * o + c : 3 * o + c + 1], (width, width))

    def counts(slot, base, peer):
        table = []
        for o in range(nb):
            row = []
            for r in range(nb):
                value = jnp.full((1, width), base, jnp.float32)
                if peer is not None:
                    sent, partner = send_ref[0, peer], partner_ref[0, peer]
                    mine = jnp.logical_and(sent == o, partner == r)
                    value = value + jnp.where(mine, 1.0, 0.0)
                    source = stage if slot is None else held
                    place = dom if slot is None else slot
                    got, for_mine = source[place, srow : srow + 1, :], source[place, prow : prow + 1, :]
                    value = value + jnp.where(
                        jnp.logical_and(got == float(r), for_mine == float(o)), 1.0, 0.0
                    )
                row.append(value)
            table.append(row)
        return table

    def fill_numer(slot, base, peer):
        where = 0 if slot is None else slot
        table = counts(slot, base, peer)
        lines = jnp.concatenate([held[where, lrow : lrow + used, :], zeros], axis=0)
        pieces = []
        for r in range(nb):
            here = jnp.logical_and(tile_row >= 3 * r, tile_row < 3 * r + 3)
            own_lines = jnp.where(here, lines, 0.0)
            b = [held[where, brow + 3 * r + a : brow + 3 * r + a + 1, :] for a in range(3)]
            pieces.append(jnp.concatenate([b[a] * own_lines for a in range(3)], axis=0))
        for o in range(nb):
            right = jnp.concatenate([pieces[r] * table[o][r] for r in range(nb)], axis=1)
            high = right.astype(jnp.bfloat16).astype(jnp.float32)
            rest = jnp.zeros((DEPTH - 72, nb * width), jnp.float32)
            stack = jnp.concatenate([high, right - high, high, rest], axis=0)
            numer[where, o] = jnp.dot(
                left_side[o], stack.astype(jnp.bfloat16), preferred_element_type=jnp.float32
            )

    def add_slot(slot, step, first=False):
        rows = []
        for r in range(nb):
            for c in range(3):
                row = held[slot, 3 * r + c : 3 * r + c + 1, :]
                if step is not None:
                    row = row + step * vel_rx[slot, r * 3 + c : r * 3 + c + 1, :]
                rows.append(jnp.broadcast_to(row, (8, width)))
        for o in range(nb):
            for g in range(width // 8):
                part = pl.ds(8 * g, 8)
                mine = [at_i[o, c, part, :] for c in range(3)]
                total = None if first else [acc[o, c, part, :] for c in range(3)]
                for r in range(nb):
                    off = [mine[c] - rows[r * 3 + c] for c in range(3)]
                    square = CORE_SQUARE + off[0] * off[0] + off[1] * off[1] + off[2] * off[2]
                    inverse = lax.rsqrt(square)
                    weight = numer[slot, o, part, pl.ds(width * r, width)] * inverse * (inverse * inverse)
                    terms = [weight * off[c] for c in range(3)]
                    total = terms if total is None else [total[c] + terms[c] for c in range(3)]
                for c in range(3):
                    acc[o, c, part, :] = total[c]

    def velocity_of(position):
        high, low = split(acc[...].reshape(used * width, width))
        lane_sums = jnp.dot(
            jnp.concatenate([high, low], axis=1),
            jnp.ones((2 * width, width), jnp.bfloat16),
            preferred_element_type=jnp.float32,
        ).reshape(used, width, width)
        sums = [
            jnp.sum(jnp.where(diagonal, lane_sums[row], 0.0), axis=0, keepdims=True) for row in range(used)
        ]
        pair = jnp.concatenate(sums + [zeros], axis=0)
        before = jnp.where(lane == 0, position, pltpu.roll(position, 1, 1))
        after = jnp.where(lane == width - 1, position, pltpu.roll(position, width - 1, 1))
        chain = before + after - 2.0 * position
        force = COUPLE * pair + applied + TENSION * chain
        velocity = force / drag
        square = velocity * velocity
        tops = []
        for o in range(nb):
            tops.append(square[3 * o : 3 * o + 1] + square[3 * o + 1 : 3 * o + 2] + square[3 * o + 2 : 3 * o + 3])
        return velocity, functools.reduce(jnp.maximum, tops)

    def step_length(row):
        top = jnp.max(row, axis=1, keepdims=True)
        return STEP_LENGTH / (jnp.sqrt(top) + EPSILON)

    fill_numer(None, 1.0, dom)
    add_slot(0, None, first=True)

    pl.semaphore_wait(barrier, slots - 1)
    repeat(1, n_dom, lambda k: dom_copy(k).start())
    repeat(1, n_sub, lambda k: sub_copy(k).start())

    def from_sub(k, carry):
        sub_copy(k).wait_recv()
        fill_numer(k, 1.0, None)
        add_slot(k, None)
        return carry

    def from_dom(k, carry):
        slot = n_sub - 1 + k
        dom_copy(k).wait_recv()
        fill_numer(slot, 0.0, lax.rem(dom - k + n_dom, n_dom))
        add_slot(slot, None)
        return carry

    lax.fori_loop(1, n_sub, from_sub, 0)
    lax.fori_loop(1, n_dom, from_dom, 0)
    velocity, top = velocity_of(position)
    vel_tx[...] = jnp.concatenate([velocity[0 : 3 * nb], top, zeros[: spare - 1]], axis=0)
    top1_tx[...] = top

    def vel_copy(slot, target):
        return pltpu.make_async_remote_copy(
            src_ref=vel_tx,
            dst_ref=vel_rx.at[slot],
            send_sem=vel_send,
            recv_sem=vel_recv,
            device_id=target,
            device_id_type=MESH,
        )

    def top1_copy(index):
        kd, ks = index // (n_sub - 1) + 1, index % (n_sub - 1) + 1
        return pltpu.make_async_remote_copy(
            src_ref=top1_tx,
            dst_ref=top1_rx.at[index],
            send_sem=top1_send,
            recv_sem=top1_recv,
            device_id=(lax.rem(dom + kd, n_dom), lax.rem(sub + ks, n_sub)),
            device_id_type=MESH,
        )

    others = (n_sub - 1) * (n_dom - 1)
    repeat(1, n_dom, lambda k: vel_copy(n_sub - 1 + k, dom_at(k)).start())
    repeat(0, others, lambda k: top1_copy(k).start())
    repeat(1, n_sub, lambda k: vel_copy(k, sub_at(k)).start())

    vel_rx[0] = vel_tx[...]
    turned = velocity.T
    for o in range(nb):
        for c in range(3):
            vel_i[o, c] = jnp.broadcast_to(turned[:, 3 * o + c : 3 * o + c + 1], (width, width))

    arrived = vel_rx.at[pl.ds(1, slots - 1)]
    pltpu.make_async_copy(arrived, arrived, vel_recv).wait()
    pltpu.make_async_copy(top1_rx, top1_rx, top1_recv).wait()
    near = jnp.max(vel_rx[:, 3 * nb : 3 * nb + 1, :], axis=0)
    far = jnp.max(top1_rx[...], axis=0)
    step = step_length(jnp.maximum(near, far))

    position = position + step * velocity

    def move(slot):
        tile = held[slot, 0:8, :] + step * vel_rx[slot]
        for row in range(used):
            sources[slot, row] = jnp.broadcast_to(tile[row : row + 1], (8, width))

    repeat(0, slots, move)

    def chunk(g, carry):
        part = pl.ds(pl.multiple_of(8 * g, 8), 8)
        mine = [[at_i[o, c, part, :] + step * vel_i[o, c, part, :] for c in range(3)] for o in range(nb)]

        def add_one(slot, total):
            total = list(total)
            for r in range(nb):
                theirs = [sources[slot, 3 * r + c] for c in range(3)]
                for o in range(nb):
                    off = [mine[o][c] - theirs[c] for c in range(3)]
                    square = CORE_SQUARE + off[0] * off[0] + off[1] * off[1] + off[2] * off[2]
                    inverse = lax.rsqrt(square)
                    weight = numer[slot, o, part, pl.ds(width * r, width)] * inverse * (inverse * inverse)
                    for c in range(3):
                        total[3 * o + c] = total[3 * o + c] + weight * off[c]
            return total

        total = [jnp.zeros((8, width), jnp.float32)] * used
        if slots <= UNROLL_LIMIT:
            for slot in range(slots):
                total = add_one(slot, total)
        else:
            total = lax.fori_loop(0, slots, add_one, total)
        for o in range(nb):
            for c in range(3):
                acc[o, c, part, :] = total[3 * o + c]
        return carry

    lax.fori_loop(0, width // 8, chunk, 0, unroll=4)
    velocity, top = velocity_of(position)
    top2_tx[...] = top

    def top2_copy(index):
        kd, ks = (index + 1) // n_sub, (index + 1) % n_sub
        return pltpu.make_async_remote_copy(
            src_ref=top2_tx,
            dst_ref=top2_rx.at[index],
            send_sem=top2_send,
            recv_sem=top2_recv,
            device_id=(lax.rem(dom + kd, n_dom), lax.rem(sub + ks, n_sub)),
            device_id_type=MESH,
        )

    repeat(0, n_sub * n_dom - 1, lambda k: top2_copy(k).start())
    for o in range(nb):
        vel_ref[o] = velocity[3 * o : 3 * o + 3]

    repeat(1, n_sub, lambda k: sub_copy(k).wait_send())
    repeat(1, n_dom, lambda k: dom_copy(k).wait_send())
    pltpu.make_async_copy(arrived, arrived, vel_send).wait()
    pltpu.make_async_copy(top1_rx, top1_rx, top1_send).wait()

    pltpu.make_async_copy(top2_rx, top2_rx, top2_recv).wait()
    step = step_length(jnp.maximum(jnp.max(top2_rx[...], axis=0), top))
    position = position + step * velocity
    for o in range(nb):
        pos_ref[o] = position[3 * o : 3 * o + 3]
    pltpu.make_async_copy(top2_rx, top2_rx, top2_send).wait()


def solution(mesh):
    n_dom, n_sub = mesh.shape["dom"], mesh.shape["sub"]

    def local(segments, stress, drag_coef, send_ids, partner_ids):
        nb, _, width = segments.shape
        slots = n_sub + n_dom - 1
        f32 = jnp.float32
        vmem = pl.BlockSpec(memory_space=pltpu.VMEM)
        smem = pl.BlockSpec(memory_space=pltpu.SMEM)
        out = jax.ShapeDtypeStruct((nb, 3, width), f32)
        rows = 9 * nb + 2
        words = 48 * slots * width + slots * nb * width * nb * width + (n_dom + slots) * (rows + 8) * width + 9 * nb * width * width
        return pl.pallas_call(
            functools.partial(kernel, n_dom, n_sub),
            out_shape=(out, out),
            in_specs=[vmem, vmem, smem, smem, smem],
            out_specs=(vmem, vmem),
            scratch_shapes=[
                pltpu.VMEM((n_dom, rows, width), f32),
                pltpu.VMEM((slots, rows, width), f32),
                pltpu.VMEM((slots, nb, width, nb * width), f32),
                pltpu.VMEM((nb, width, DEPTH), jnp.bfloat16),
                pltpu.VMEM((nb, 3, width, width), f32),
                pltpu.VMEM((nb, 3, width, width), f32),
                pltpu.VMEM((nb, 3, width, width), f32),
                pltpu.VMEM((slots, 3 * nb, 8, width), f32),
                pltpu.VMEM((8, width), f32),
                pltpu.VMEM((slots, 8, width), f32),
                pltpu.VMEM((1, width), f32),
                pltpu.VMEM(((n_dom - 1) * (n_sub - 1), 1, width), f32),
                pltpu.VMEM((1, width), f32),
                pltpu.VMEM((n_dom * n_sub - 1, 1, width), f32),
                pltpu.SemaphoreType.DMA((slots,)),
                pltpu.SemaphoreType.DMA((slots,)),
                pltpu.SemaphoreType.DMA,
                pltpu.SemaphoreType.DMA,
                pltpu.SemaphoreType.DMA,
                pltpu.SemaphoreType.DMA,
                pltpu.SemaphoreType.DMA,
                pltpu.SemaphoreType.DMA,
            ],
            compiler_params=pltpu.CompilerParams(
                collective_id=0,
                has_side_effects=True,
                vmem_limit_bytes=4 * words + 8 * 1024 * 1024,
            ),
        )(
            segments,
            drag_coef,
            stress,
            send_ids.reshape(1, n_dom),
            partner_ids.reshape(1, n_dom),
        )

    in_specs = (
        P(("dom", "sub"), None, None),
        P(),
        P(("dom", "sub"), None),
        P(("dom", "sub"), None, None),
        P(("dom", "sub"), None, None),
    )
    out_specs = (P(("dom", "sub"), None, None), P(("dom", "sub"), None, None))
    return jax.shard_map(local, mesh=mesh, in_specs=in_specs, out_specs=out_specs, check_vma=False)
```
